128 devices in a mesh: row: 8 (over z, y_lo), col: 16 (over x, y_hi, core).
Axes of the slice: x: 4, y: 4 (y_hi: 2, y_lo: 2; y = y_hi * 2 + y_lo), z: 4, core: 2. Of those that a mesh axis runs over, the one named last changes fastest.
Arguments:
- pair_input: bfloat16 [384, 384, 128], P('row', 'col'), may hold values from -6 to 6
- chain_lengths: int32 [8], replicated, may hold values from 24 to 48, as said below
- input_gain: float32 [2, 128], replicated, may hold values from 0.1 to 1.9
- input_weight: bfloat16 [2, 128, 640], replicated, may hold values from -0.5 to 0.5
- output_gain: float32 [2, 128], replicated, may hold values from 0.1 to 1.9
- output_weight: bfloat16 [2, 128, 128], replicated, may hold values from -0.5 to 0.5
- cotangent: bfloat16 [384, 384, 128], P('row', 'col'), may hold values from -6 to 6
Outputs:
- pair_output: bfloat16 [384, 384, 128], P('row', 'col')
- pair_grad: float32 [384, 384, 128], P('row', 'col')
The draws below stay inside these ranges and needn't reach their ends.
Inputs may be any that keep to these rules, and one draw needn't show every extreme that they name: `chain_lengths`: every chain has at least half of its 48 positions valid; in every draw at least one chain is entirely valid and one exactly half valid.
All inputs are finite; a program needn't handle non-finite values.
Results may differ from the reference program's by a relative error of at most 0.025.
Values may be sent and summed in bfloat16 or wider, within the bound.
A program may use at most 128 MiB of HBM per device.

```python
import jax
import jax.numpy as jnp
from jax import lax

CZ = 128
CH = 128
N = 384
CHAINS = 8


def draw_chain_lengths(key, part):
    key = jax.random.fold_in(key, 11)
    key_values, key_ranking = jax.random.split(key)
    stride = N // CHAINS
    lengths_drawn = jax.random.randint(key_values, (CHAINS,), stride // 2, stride + 1, dtype=jnp.int32)
    ranking = jax.random.permutation(key_ranking, CHAINS)
    lengths_drawn = lengths_drawn.at[ranking[0]].set(stride).at[ranking[1]].set(stride // 2)
    return lengths_drawn.astype(jnp.int32)


def block_levels(rng, shape, shards, least, top_value):
    gain = 1.0
    for dim, shards_of in shards:
        draws = jax.random.uniform(jax.random.fold_in(jax.random.fold_in(rng, 6), dim), (shards_of,), jnp.float32, least / len(shards), top_value / len(shards))
        gain = gain * jnp.repeat(jnp.exp(draws), shape[dim] // shards_of).reshape((-1,) + (1,) * (len(shape) - 1 - dim))
    return gain


def noise(own_key, extent, scale, bound, shards=(), kind=jnp.bfloat16):
    array = jax.random.normal(own_key, extent, jnp.float32) * scale
    if len(shards) > 0:
        array = block_levels(own_key, extent, shards, -0.22, 0.18) * array
    return jnp.clip(array, min=-bound, max=bound).astype(kind)


def setup_inputs(seed: int = 0) -> dict:
    streams_of = jax.random.split(jax.random.key(seed), 8)
    pair_input = noise(streams_of[0], (N, N, CZ), 1.0, 6.0, ((0, 8), (1, 16)))
    chain_lengths = draw_chain_lengths(jax.random.fold_in(streams_of[7], 71), 0)
    input_gain = jnp.clip(1.0 + 0.18 * jax.random.normal(streams_of[2], (2, CZ), jnp.float32), 0.1, 1.9)
    input_weight = noise(streams_of[3], (2, CZ, 4 * CH + CZ), CZ ** -0.5, 0.5)
    output_gain = jnp.clip(1.0 + 0.18 * jax.random.normal(streams_of[4], (2, CH), jnp.float32), 0.1, 1.9)
    output_weight = noise(streams_of[5], (2, CH, CZ), CH ** -0.5, 0.5)
    cotangent = noise(streams_of[6], (N, N, CZ), 1.0, 6.0, ((0, 8), (1, 16)))
    return dict(pair_input=pair_input, chain_lengths=chain_lengths, input_gain=input_gain, input_weight=input_weight, output_gain=output_gain, output_weight=output_weight, cotangent=cotangent)


EPSILON = 1e-05

def normalize(values):
    center = values - lax.optimization_barrier(jnp.mean(values, axis=-1, keepdims=True))
    inverse = lax.rsqrt(lax.optimization_barrier(jnp.mean(center * center, axis=-1, keepdims=True)) + EPSILON)
    return (center * inverse, inverse)

def norm_backward(grad_normed, normed, inverse):
    return inverse * (grad_normed - lax.optimization_barrier(jnp.mean(grad_normed, axis=-1, keepdims=True)) - normed * lax.optimization_barrier(jnp.mean(grad_normed * normed, axis=-1, keepdims=True)))

def token_valid(chain_lengths, offset, amount):
    positions = offset + jnp.arange(amount, dtype=jnp.int32)
    stride = N // CHAINS
    chain_index = positions // stride
    chosen = lax.optimization_barrier(jnp.sum(jnp.where(chain_index[:, None] == jnp.arange(CHAINS, dtype=jnp.int32)[None, :], chain_lengths[None, :], 0), axis=1))
    return (positions % stride < chosen).astype(jnp.float32)

def project_pair(pair_state, norm_gain, weight, pair_mask):
    normed, inverse = normalize(pair_state.astype(jnp.float32))
    scaled = (normed * norm_gain).astype(jnp.bfloat16)
    mixed_all = jnp.dot(scaled, weight, preferred_element_type=jnp.float32)
    mask_cells = pair_mask[:, :, None]
    left_side = (jax.nn.sigmoid(mixed_all[..., CH:2 * CH]) * mixed_all[..., :CH] * mask_cells).astype(jnp.bfloat16)
    right_side = (jax.nn.sigmoid(mixed_all[..., 3 * CH:4 * CH]) * mixed_all[..., 2 * CH:3 * CH] * mask_cells).astype(jnp.bfloat16)
    return (mixed_all, left_side, right_side)

def finish_pair(pair_state, product, norm_gain, weight, mixed_all):
    normed, inverse = normalize(product)
    scaled = (normed * norm_gain).astype(jnp.bfloat16)
    projected = jnp.dot(scaled, weight, preferred_element_type=jnp.float32)
    return (pair_state.astype(jnp.float32) + jax.nn.sigmoid(mixed_all[..., 4 * CH:]) * projected).astype(jnp.bfloat16)

def finish_back(upstream, product, norm_gain, weight, mixed_all):
    normed, inverse = normalize(product)
    scaled = (normed * norm_gain).astype(jnp.bfloat16)
    projected = jnp.dot(scaled, weight, preferred_element_type=jnp.float32)
    gate_value = jax.nn.sigmoid(mixed_all[..., 4 * CH:])
    grad_projected = (upstream * gate_value).astype(jnp.bfloat16)
    grad_gate = upstream * projected * gate_value * (1.0 - gate_value)
    grad_scaled = jnp.dot(grad_projected, weight.T, preferred_element_type=jnp.float32)
    grad_product = norm_backward(grad_scaled * norm_gain, normed, inverse)
    return (grad_product.astype(jnp.bfloat16), grad_gate)

def project_back(grad_left, grad_right, grad_gate, pair_state, norm_gain, weight, pair_mask):
    normed, inverse = normalize(pair_state.astype(jnp.float32))
    scaled = (normed * norm_gain).astype(jnp.bfloat16)
    mixed_all = jnp.dot(scaled, weight, preferred_element_type=jnp.float32)
    mask_cells = pair_mask[:, :, None]
    left_gate = jax.nn.sigmoid(mixed_all[..., CH:2 * CH])
    right_gate = jax.nn.sigmoid(mixed_all[..., 3 * CH:4 * CH])
    grad_mixed = jnp.concatenate([grad_left * left_gate * mask_cells, grad_left * mixed_all[..., :CH] * mask_cells * left_gate * (1.0 - left_gate), grad_right * right_gate * mask_cells, grad_right * mixed_all[..., 2 * CH:3 * CH] * mask_cells * right_gate * (1.0 - right_gate), grad_gate], axis=-1).astype(jnp.bfloat16)
    grad_scaled = jnp.dot(grad_mixed, weight.T, preferred_element_type=jnp.float32)
    return norm_backward(grad_scaled * norm_gain, normed, inverse)

def contract(form, first, second):
    return jnp.einsum(form, first.astype(jnp.float32), second.astype(jnp.float32), precision=lax.Precision.HIGHEST)

def reference(pair_input, chain_lengths, input_gain, input_weight, output_gain, output_weight, cotangent):
    valid = token_valid(chain_lengths, 0, N)
    pair_mask = valid[:, None] * valid[None, :]
    mixed_out, left_out, right_out = project_pair(pair_input, input_gain[0], input_weight[0], pair_mask)
    product_out = contract('ikc,jkc->ijc', left_out, right_out)
    pair_mid = finish_pair(pair_input, product_out, output_gain[0], output_weight[0], mixed_out)
    mixed_in, left_in, right_in = project_pair(pair_mid, input_gain[1], input_weight[1], pair_mask)
    product_in = contract('kic,kjc->ijc', left_in, right_in)
    pair_output = finish_pair(pair_mid, product_in, output_gain[1], output_weight[1], mixed_in)
    upstream = cotangent.astype(jnp.float32)
    grad_in, gate_in = finish_back(upstream, product_in, output_gain[1], output_weight[1], mixed_in)
    grad_left_in = contract('ijc,kjc->kic', grad_in, right_in)
    grad_right_in = contract('ijc,kic->kjc', grad_in, left_in)
    upstream_mid = upstream + project_back(grad_left_in, grad_right_in, gate_in, pair_mid, input_gain[1], input_weight[1], pair_mask)
    grad_out, gate_out = finish_back(upstream_mid, product_out, output_gain[0], output_weight[0], mixed_out)
    grad_left_out = contract('ijc,jkc->ikc', grad_out, right_out)
    grad_right_out = contract('ijc,ikc->jkc', grad_out, left_out)
    pair_grad = upstream_mid + project_back(grad_left_out, grad_right_out, gate_out, pair_input, input_gain[0], input_weight[0], pair_mask)
    return (pair_output, pair_grad)
```

```python
import jax
import jax.numpy as jnp
from jax import lax
from jax.sharding import PartitionSpec as P

CH = 128
N = 384
CHAINS = 8


EPSILON = 1e-05


def normalize(values):
    center = values - jnp.mean(values, axis=-1, keepdims=True)
    inverse = lax.rsqrt(jnp.mean(center * center, axis=-1, keepdims=True) + EPSILON)
    return (center * inverse, inverse)


def norm_backward(grad_normed, normed, inverse):
    return inverse * (
        grad_normed
        - jnp.mean(grad_normed, axis=-1, keepdims=True)
        - normed * jnp.mean(grad_normed * normed, axis=-1, keepdims=True)
    )


def token_valid(chain_lengths, offset, amount):
    positions = offset + jnp.arange(amount, dtype=jnp.int32)
    stride = N // CHAINS
    chain_index = positions // stride
    chosen = jnp.sum(
        jnp.where(
            chain_index[:, None] == jnp.arange(CHAINS, dtype=jnp.int32)[None, :],
            chain_lengths[None, :],
            0,
        ),
        axis=1,
    )
    return (positions % stride < chosen).astype(jnp.float32)


def project_pair(pair_state, norm_gain, weight, pair_mask):
    normed, inverse = normalize(pair_state.astype(jnp.float32))
    scaled = (normed * norm_gain).astype(jnp.bfloat16)
    mixed_all = jnp.dot(scaled, weight, preferred_element_type=jnp.float32)
    mask_cells = pair_mask[:, :, None]
    left_side = (
        jax.nn.sigmoid(mixed_all[..., CH : 2 * CH]) * mixed_all[..., :CH] * mask_cells
    ).astype(jnp.bfloat16)
    right_side = (
        jax.nn.sigmoid(mixed_all[..., 3 * CH : 4 * CH])
        * mixed_all[..., 2 * CH : 3 * CH]
        * mask_cells
    ).astype(jnp.bfloat16)
    return (mixed_all, left_side, right_side)


def finish_pair(pair_state, product, norm_gain, weight, mixed_all):
    normed, inverse = normalize(product)
    scaled = (normed * norm_gain).astype(jnp.bfloat16)
    projected = jnp.dot(scaled, weight, preferred_element_type=jnp.float32)
    return (
        pair_state.astype(jnp.float32) + jax.nn.sigmoid(mixed_all[..., 4 * CH :]) * projected
    ).astype(jnp.bfloat16)


def finish_back(upstream, product, norm_gain, weight, mixed_all):
    normed, inverse = normalize(product)
    scaled = (normed * norm_gain).astype(jnp.bfloat16)
    projected = jnp.dot(scaled, weight, preferred_element_type=jnp.float32)
    gate_value = jax.nn.sigmoid(mixed_all[..., 4 * CH :])
    grad_projected = (upstream * gate_value).astype(jnp.bfloat16)
    grad_gate = upstream * projected * gate_value * (1.0 - gate_value)
    grad_scaled = jnp.dot(grad_projected, weight.T, preferred_element_type=jnp.float32)
    grad_product = norm_backward(grad_scaled * norm_gain, normed, inverse)
    return (grad_product.astype(jnp.bfloat16), grad_gate)


def project_back(grad_left, grad_right, grad_gate, pair_state, norm_gain, weight, pair_mask):
    normed, inverse = normalize(pair_state.astype(jnp.float32))
    scaled = (normed * norm_gain).astype(jnp.bfloat16)
    mixed_all = jnp.dot(scaled, weight, preferred_element_type=jnp.float32)
    mask_cells = pair_mask[:, :, None]
    left_gate = jax.nn.sigmoid(mixed_all[..., CH : 2 * CH])
    right_gate = jax.nn.sigmoid(mixed_all[..., 3 * CH : 4 * CH])
    grad_mixed = jnp.concatenate(
        [
            grad_left * left_gate * mask_cells,
            grad_left * mixed_all[..., :CH] * mask_cells * left_gate * (1.0 - left_gate),
            grad_right * right_gate * mask_cells,
            grad_right
            * mixed_all[..., 2 * CH : 3 * CH]
            * mask_cells
            * right_gate
            * (1.0 - right_gate),
            grad_gate,
        ],
        axis=-1,
    ).astype(jnp.bfloat16)
    grad_scaled = jnp.dot(grad_mixed, weight.T, preferred_element_type=jnp.float32)
    return norm_backward(grad_scaled * norm_gain, normed, inverse)


AXES = ("row", "col")


def to_channels(*parts):
    rows, columns, channels = parts[0].shape
    packed = jnp.stack([p.reshape(rows * columns, channels).T for p in parts], axis=1)
    moved = lax.all_to_all(packed, AXES, split_axis=0, concat_axis=0, tiled=True)
    grid = moved.reshape(lax.axis_size("row"), lax.axis_size("col"), len(parts), rows, columns)
    grid = grid.transpose(2, 0, 3, 1, 4)
    return [grid[i].reshape(N, N) for i in range(len(parts))]


def to_blocks(*parts):
    across, down = lax.axis_size("row"), lax.axis_size("col")
    rows, columns = N // across, N // down
    packed = jnp.stack(parts).astype(jnp.bfloat16)
    packed = packed.reshape(len(parts), across, rows, down, columns).transpose(1, 3, 0, 2, 4)
    packed = packed.reshape(across * down, len(parts), rows * columns)
    moved = lax.all_to_all(packed, AXES, split_axis=0, concat_axis=0, tiled=True)
    return [
        moved[:, i].T.reshape(rows, columns, -1).astype(jnp.float32) for i in range(len(parts))
    ]


def multiply(form, first, second):
    return jnp.einsum(form, first, second, preferred_element_type=jnp.float32)


def local(
    pair_input, chain_lengths, input_gain, input_weight, output_gain, output_weight, cotangent
):
    row_count = pair_input.shape[0]
    column_count = pair_input.shape[1]
    row_valid = token_valid(chain_lengths, lax.axis_index("row") * row_count, row_count)
    column_valid = token_valid(chain_lengths, lax.axis_index("col") * column_count, column_count)
    pair_mask = row_valid[:, None] * column_valid[None, :]
    mixed_out, left_out, right_out = project_pair(
        pair_input, input_gain[0], input_weight[0], pair_mask
    )
    left_0, right_0 = to_channels(left_out, right_out)
    (product_out,) = to_blocks(multiply("ik,jk->ij", left_0, right_0))
    pair_mid = finish_pair(pair_input, product_out, output_gain[0], output_weight[0], mixed_out)
    mixed_in, left_in, right_in = project_pair(pair_mid, input_gain[1], input_weight[1], pair_mask)
    left_1, right_1 = to_channels(left_in, right_in)
    (product_in,) = to_blocks(multiply("ki,kj->ij", left_1, right_1))
    pair_output = finish_pair(pair_mid, product_in, output_gain[1], output_weight[1], mixed_in)
    upstream = cotangent.astype(jnp.float32)
    grad_in, gate_in = finish_back(upstream, product_in, output_gain[1], output_weight[1], mixed_in)
    (grad_1,) = to_channels(grad_in)
    grad_left_in, grad_right_in = to_blocks(
        multiply("ij,kj->ki", grad_1, right_1), multiply("ij,ki->kj", grad_1, left_1)
    )
    upstream_mid = upstream + project_back(
        grad_left_in, grad_right_in, gate_in, pair_mid, input_gain[1], input_weight[1], pair_mask
    )
    grad_out, gate_out = finish_back(
        upstream_mid, product_out, output_gain[0], output_weight[0], mixed_out
    )
    (grad_0,) = to_channels(grad_out)
    grad_left_out, grad_right_out = to_blocks(
        multiply("ij,jk->ik", grad_0, right_0), multiply("ij,ik->jk", grad_0, left_0)
    )
    pair_grad = upstream_mid + project_back(
        grad_left_out,
        grad_right_out,
        gate_out,
        pair_input,
        input_gain[0],
        input_weight[0],
        pair_mask,
    )
    return (pair_output, pair_grad)


def solution(mesh):
    placed = (P("row", "col", None), P(), P(), P(), P(), P(), P("row", "col", None))
    return jax.shard_map(
        local,
        mesh=mesh,
        in_specs=placed,
        out_specs=(P("row", "col", None), P("row", "col", None)),
        check_vma=False,
    )
```

```python
import functools

import jax
import jax.numpy as jnp
from jax import lax
from jax.experimental import pallas as pl
from jax.experimental.pallas import tpu as pltpu
from jax.sharding import PartitionSpec as P

MESH = pl.DeviceIdType.MESH
F32 = jnp.float32
BF16 = jnp.bfloat16

CH = 128
N = 384
CHAINS = 8
EPSILON = 1e-05

ROWS, COLS = 8, 16
DEVICES = ROWS * COLS
HEIGHT, WIDTH = N // ROWS, N // COLS
HALF = 64
TILES = WIDTH // 2
LANES = TILES * 128
STEP = 256
STEPS = LANES // STEP
SIDE = CHAINS * HALF


def column_pair(tile):
    return (tile, tile + 8) if tile < 8 else (tile + 8, tile + 12)


def sigmoid(values):
    return 0.5 * jnp.tanh(0.5 * values) + 0.5


def mean_rows(values):
    return jnp.sum(values, axis=0, keepdims=True) * (1.0 / values.shape[0])


def normalize(values):
    center = values - mean_rows(values)
    inverse = lax.rsqrt(mean_rows(center * center) + EPSILON)
    return center * inverse, inverse


def norm_backward(grad_normed, normed, inverse):
    return inverse * (
        grad_normed - mean_rows(grad_normed) - normed * mean_rows(grad_normed * normed)
    )


def dot(first, second, first_dim=1, second_dim=0):
    return lax.dot_general(
        first, second, (((first_dim,), (second_dim,)), ((), ())), preferred_element_type=F32
    )


def swap_halves(values):
    return pltpu.roll(values, HALF, axis=len(values.shape) - 1)


def lower_lanes(shape):
    return lax.broadcasted_iota(jnp.int32, shape, len(shape) - 1) % 128 < HALF


def merge(first, second):
    lower = lower_lanes(first.shape)
    return (
        jnp.where(lower, first, swap_halves(second)),
        jnp.where(lower, swap_halves(first), second),
    )


def kernel(
    x_ref,
    length_ref,
    ig_ref,
    iw_ref,
    og_ref,
    ow_ref,
    ct_ref,
    out_ref,
    grad_ref,
    flat,
    state,
    upstream,
    mixed,
    norm_in,
    inverse_in,
    norm_out,
    inverse_out,
    projected,
    swap,
    gains,
    weight_t,
    out_weight_t,
    left,
    right,
    grad,
    result,
    send_wide,
    send_slim,
    wide_0,
    wide_1,
    wide_2,
    wide_3,
    slim_0,
    slim_1,
    slim_2,
    slim_3,
    send_sem,
    recv_sem,
):
    row, col = lax.axis_index("row"), lax.axis_index("col")
    me = row * COLS + col

    barrier = pltpu.get_barrier_semaphore()

    def greet(t, carry):
        peer = (lax.rem(row + t // COLS, ROWS), lax.rem(col + t % COLS, COLS))
        pl.semaphore_signal(barrier, inc=1, device_id=peer, device_id_type=MESH)
        return carry

    lax.fori_loop(1, DEVICES, greet, 0)

    def send(phase, source, target):
        def one(t, carry):
            offset = lax.rem(t * 9, DEVICES)
            peer = (lax.rem(row + offset // COLS, ROWS), lax.rem(col + offset % COLS, COLS))
            pltpu.make_async_remote_copy(
                source.at[peer[0] * COLS + peer[1]],
                target.at[me],
                send_sem.at[phase],
                recv_sem.at[phase],
                device_id=peer,
                device_id_type=MESH,
            ).start()
            return carry

        lax.fori_loop(1, DEVICES, one, 0)
        target[me] = source[me]

    def receive(phase, source, target):
        others = pl.ds(0, DEVICES - 1)
        copies = pltpu.make_async_remote_copy(
            source.at[others],
            target.at[others],
            send_sem.at[phase],
            recv_sem.at[phase],
            device_id=(row, col),
            device_id_type=MESH,
        )
        copies.wait_send()
        copies.wait_recv()

    def steps(body):
        def one(s, carry):
            body(pl.ds(pl.multiple_of(s * STEP, STEP), STEP))
            return carry

        lax.fori_loop(0, STEPS, one, 0)

    def valid(at):
        lane = lax.broadcasted_iota(jnp.int32, (1, STEP), 1) + at.start
        tile = lane // 128
        token = lane % HALF
        upper = (lane // HALF) % 2
        column = tile + jnp.where(tile < 8, 8 * upper, 8 + 4 * upper) + (col % 2) * WIDTH
        inside = (token < length_ref[row]) & (column < length_ref[col // 2])
        return jnp.where(inside, 1.0, 0.0)

    def load_block(source, target):
        flat[...] = source[...].astype(F32)
        empty = jnp.zeros((HALF - HEIGHT, CH), F32)
        for tile in range(TILES):
            parts = []
            for column in column_pair(tile):
                parts += [flat[pl.ds(column, HEIGHT, stride=WIDTH), :], empty]
            target[:, tile * 128 : (tile + 1) * 128] = jnp.concatenate(parts, axis=0).T

    def store_block(source, target):
        for tile in range(TILES):
            block = source[:, tile * 128 : (tile + 1) * 128].T
            for half, column in enumerate(column_pair(tile)):
                target[pl.ds(column, HEIGHT, stride=WIDTH), :] = block[
                    half * HALF : half * HALF + HEIGHT
                ]

    def project(u):
        def body(at):
            normed, inverse = normalize(state[:, at])
            norm_in[u, :, at] = normed
            inverse_in[u, :, at] = inverse
            scaled = (normed * gains[u]).astype(BF16)
            mixed[u, :, at] = dot(weight_t[u], scaled)

        steps(body)

    def pack_wide(first, second):
        for tile in range(TILES):
            at = pl.ds(tile * 128, 128)
            lower, upper = merge(first(at), second(at))
            one, two = column_pair(tile)
            swap[pl.ds(one, CH, stride=WIDTH), :] = lower
            swap[pl.ds(two, CH, stride=WIDTH), :] = upper

        def one(c, carry):
            at = pl.ds(pl.multiple_of(c * 16 * WIDTH, 16 * WIDTH), 16 * WIDTH)
            send_wide[pl.ds(c * 16, 16)] = swap[at, :].astype(BF16).reshape(16, WIDTH, 128)
            return carry

        lax.fori_loop(0, CH // 16, one, 0)

    def unpack(source, rows):
        def one(c, carry):
            at = pl.ds(pl.multiple_of(c * 16 * rows, 16 * rows), 16 * rows)
            swap[at, :] = source[pl.ds(c * 16, 16)].astype(F32).reshape(16 * rows, 128)
            return carry

        lax.fori_loop(0, CH // 16, one, 0)

    def pack_slim(first):
        for tile in range(TILES):
            swap[pl.ds(tile, CH, stride=16), :] = first[:, tile * 128 : (tile + 1) * 128]

        def one(c, carry):
            at = pl.ds(pl.multiple_of(c * 256, 256), 256)
            send_slim[pl.ds(c * 16, 16)] = swap[at, :].astype(BF16).reshape(16, 16, 128)
            return carry

        lax.fori_loop(0, CH // 16, one, 0)

    def edges(u):
        def body(at):
            keep = valid(at)
            norm_out[u, :, at] = (
                sigmoid(mixed[u, CH : 2 * CH, at]) * mixed[u, 0:CH, at] * keep
            )
            projected[u, :, at] = (
                sigmoid(mixed[u, 3 * CH : 4 * CH, at]) * mixed[u, 2 * CH : 3 * CH, at] * keep
            )

        steps(body)
        pack_wide(lambda at: norm_out[u, :, at], lambda at: projected[u, :, at])

    def blocks(body):
        def one(s, carry):
            chain = s // 4
            pair = s % 4
            body(
                chain,
                pair,
                pl.ds(pl.multiple_of(chain * HALF, HALF), HALF),
                pl.ds(pl.multiple_of(pair * 128, 128), 128),
            )
            return carry

        lax.fori_loop(0, CHAINS * 4, one, 0)

    def assemble_wide(source, first, second):
        def body(chain, pair, down, across):
            firsts, seconds = [], []
            for part in range(2):
                at = pair * 2 * COLS + chain * 2 + part
                one, two = merge(source[at].astype(F32), source[at + COLS].astype(F32))
                firsts.append(one)
                seconds.append(two)
            empty = jnp.zeros((HALF - 2 * WIDTH, 128), F32)
            first[down, across] = jnp.concatenate(firsts + [empty], axis=0).astype(BF16)
            second[down, across] = jnp.concatenate(seconds + [empty], axis=0).astype(BF16)

        blocks(body)

    def assemble_slim(source, target):
        def body(chain, pair, down, across):
            parts = []
            for part in range(2):
                at = pair * 2 * COLS + chain * 2 + part
                one, two = merge(source[at].astype(F32), source[at + COLS].astype(F32))
                low = lax.broadcasted_iota(jnp.int32, (8, 128), 0) < 4
                last = jnp.where(low, one[8:16], pltpu.roll(two[8:16], 4, axis=0))
                parts += [one[0:8], two[0:8], last]
            empty = jnp.zeros((HALF - 2 * WIDTH, 128), F32)
            target[down, across] = jnp.concatenate(parts + [empty], axis=0).astype(BF16)

        blocks(body)

    def split_wide(first, second):
        def body(chain, pair, down, across):
            lower, upper = merge(first[down, across], second[down, across])
            for part in range(2):
                at = pair * 2 * COLS + chain * 2 + part
                cut = slice(part * WIDTH, (part + 1) * WIDTH)
                send_wide[at] = lower[cut].astype(BF16)
                send_wide[at + COLS] = upper[cut].astype(BF16)

        blocks(body)

    def split_slim(source):
        def body(chain, pair, down, across):
            values = source[down, across]
            for part in range(2):
                at = pair * 2 * COLS + chain * 2 + part
                cut = values[part * WIDTH : (part + 1) * WIDTH]
                last = cut[16:24]
                low_0, low_1 = merge(cut[0:8], cut[8:16])
                high_0, high_1 = merge(last, pltpu.roll(last, 4, axis=0))
                send_slim[at] = jnp.concatenate([low_0, high_0], axis=0).astype(BF16)
                send_slim[at + COLS] = jnp.concatenate([low_1, high_1], axis=0).astype(BF16)

        blocks(body)

    def finish(u, source):
        unpack(source, 16)
        for tile in range(TILES):
            norm_out[u, :, tile * 128 : (tile + 1) * 128] = swap[pl.ds(tile, CH, stride=16), :]

        def body(at):
            normed, inverse = normalize(norm_out[u, :, at])
            norm_out[u, :, at] = normed
            inverse_out[u, :, at] = inverse
            scaled = (normed * gains[2 + u]).astype(BF16)
            values = dot(out_weight_t[u], scaled)
            projected[u, :, at] = values
            gate = sigmoid(mixed[u, 4 * CH :, at])
            state[:, at] = (state[:, at] + gate * values).astype(BF16).astype(F32)

        steps(body)

    def finish_back(u):
        def body(at):
            up = upstream[:, at]
            gate = sigmoid(mixed[u, 4 * CH :, at])
            grad_projected = up * gate
            mixed[u, 4 * CH :, at] = grad_projected * projected[u, :, at] * (1.0 - gate)
            grad_scaled = dot(ow_ref[u], grad_projected.astype(BF16))
            projected[u, :, at] = norm_backward(
                grad_scaled * gains[2 + u], norm_out[u, :, at], inverse_out[u, :, at]
            )

        steps(body)
        pack_slim(projected.at[u])

    def project_back(u, source):
        unpack(source, WIDTH)
        for tile in range(TILES):
            at = slice(tile * 128, (tile + 1) * 128)
            one, two = column_pair(tile)
            lower, upper = merge(
                swap[pl.ds(one, CH, stride=WIDTH), :], swap[pl.ds(two, CH, stride=WIDTH), :]
            )
            norm_out[u, :, at] = lower
            projected[u, :, at] = upper

        def body(at):
            keep = valid(at)
            parts = []
            for values, base in ((norm_out, 0), (projected, 2 * CH)):
                gate = sigmoid(mixed[u, base + CH : base + 2 * CH, at])
                direct = values[u, :, at] * gate * keep
                parts.append(direct.astype(BF16))
                parts.append((direct * mixed[u, base : base + CH, at] * (1.0 - gate)).astype(BF16))
            parts.append(mixed[u, 4 * CH :, at].astype(BF16))
            grad_scaled = dot(iw_ref[u], jnp.concatenate(parts, axis=0))
            upstream[:, at] = upstream[:, at] + norm_backward(
                grad_scaled * gains[u], norm_in[u, :, at], inverse_in[u, :, at]
            )

        steps(body)

    for u in range(2):
        weight_t[u] = iw_ref[u].astype(F32).T.astype(BF16)
        out_weight_t[u] = ow_ref[u].astype(F32).T.astype(BF16)
        for i, ref in ((u, ig_ref), (2 + u, og_ref)):
            spread = jnp.broadcast_to(ref[u : u + 1, :], (CH, CH)).T
            gains[i] = jnp.concatenate([spread, spread], axis=1)

    load_block(x_ref, state)
    project(0)
    edges(0)
    pl.semaphore_wait(barrier, DEVICES - 1)
    send(0, send_wide, wide_0)
    load_block(ct_ref, upstream)
    receive(0, send_wide, wide_0)
    assemble_wide(wide_0, left.at[0], right.at[0])
    result[0] = dot(right[0], left[0], 0, 0)
    split_slim(result.at[0])
    send(1, send_slim, slim_0)
    receive(1, send_slim, slim_0)

    finish(0, slim_0)
    project(1)
    edges(1)
    send(2, send_wide, wide_1)
    receive(2, send_wide, wide_1)
    assemble_wide(wide_1, left.at[1], right.at[1])
    result[0] = dot(right[1], left[1], 1, 1)
    split_slim(result.at[0])
    send(3, send_slim, slim_1)
    receive(3, send_slim, slim_1)

    finish(1, slim_1)
    finish_back(1)
    send(4, send_slim, slim_2)
    store_block(state, flat)
    out_ref[...] = flat[...].astype(BF16)
    receive(4, send_slim, slim_2)
    assemble_slim(slim_2, grad)
    result[0] = dot(grad[...], right[1], 0, 0)
    result[1] = dot(grad[...], left[1], 1, 0)
    split_wide(result.at[0], result.at[1])
    send(5, send_wide, wide_2)
    receive(5, send_wide, wide_2)

    project_back(1, wide_2)
    finish_back(0)
    send(6, send_slim, slim_3)
    receive(6, send_slim, slim_3)
    assemble_slim(slim_3, grad)
    result[0] = dot(right[0], grad[...], 1, 0)
    result[1] = dot(left[0], grad[...], 1, 1)
    split_wide(result.at[0], result.at[1])
    send(7, send_wide, wide_3)
    receive(7, send_wide, wide_3)

    project_back(0, wide_3)
    store_block(upstream, grad_ref)


def local(
    pair_input, chain_lengths, input_gain, input_weight, output_gain, output_weight, cotangent
):
    cells = HEIGHT * WIDTH
    vmem = pl.BlockSpec(memory_space=pltpu.VMEM)
    smem = pl.BlockSpec(memory_space=pltpu.SMEM)
    wide = pltpu.VMEM((DEVICES, WIDTH, 128), BF16)
    slim = pltpu.VMEM((DEVICES, 16, 128), BF16)
    plane = pltpu.VMEM((CH, LANES), F32)
    planes = pltpu.VMEM((2, CH, LANES), F32)
    line = pltpu.VMEM((2, 1, LANES), F32)
    out, grad = pl.pallas_call(
        kernel,
        out_shape=(
            jax.ShapeDtypeStruct((cells, CH), BF16),
            jax.ShapeDtypeStruct((cells, CH), F32),
        ),
        in_specs=[vmem, smem, vmem, vmem, vmem, vmem, vmem],
        out_specs=(vmem, vmem),
        scratch_shapes=[
            pltpu.VMEM((cells, CH), F32),
            plane,
            plane,
            pltpu.VMEM((2, 5 * CH, LANES), F32),
            planes,
            line,
            planes,
            line,
            planes,
            pltpu.VMEM((CH * WIDTH, 128), F32),
            pltpu.VMEM((4, CH, STEP), F32),
            pltpu.VMEM((2, 5 * CH, CH), BF16),
            pltpu.VMEM((2, CH, CH), BF16),
            pltpu.VMEM((2, SIDE, SIDE), BF16),
            pltpu.VMEM((2, SIDE, SIDE), BF16),
            pltpu.VMEM((SIDE, SIDE), BF16),
            pltpu.VMEM((2, SIDE, SIDE), F32),
            wide,
            slim,
            wide,
            wide,
            wide,
            wide,
            slim,
            slim,
            slim,
            slim,
            pltpu.SemaphoreType.DMA((8,)),
            pltpu.SemaphoreType.DMA((8,)),
        ],
        compiler_params=pltpu.CompilerParams(
            collective_id=0, has_side_effects=True, vmem_limit_bytes=52 * 2**20
        ),
    )(
        pair_input.reshape(cells, CH),
        chain_lengths,
        input_gain,
        input_weight,
        output_gain,
        output_weight,
        cotangent.reshape(cells, CH),
    )
    shape = (HEIGHT, WIDTH, CH)
    return out.reshape(shape), grad.reshape(shape)


def solution(mesh):
    placed = (P("row", "col", None), P(), P(), P(), P(), P(), P("row", "col", None))
    return jax.shard_map(
        local,
        mesh=mesh,
        in_specs=placed,
        out_specs=(P("row", "col", None), P("row", "col", None)),
        check_vma=False,
    )
```

```python
import functools

import jax
import jax.numpy as jnp
from jax import lax
from jax.experimental import pallas as pl
from jax.experimental.pallas import tpu as pltpu
from jax.sharding import PartitionSpec as P

MESH = pl.DeviceIdType.MESH
F32 = jnp.float32
BF16 = jnp.bfloat16

CH = 128
N = 384
CHAINS = 8
EPSILON = 1e-05

ROWS, COLS = 8, 16
DEVICES = ROWS * COLS
HEIGHT, WIDTH = N // ROWS, N // COLS
HALF = 64
TILES = WIDTH // 2
LANES = TILES * 128
STEP = 256
STEPS = LANES // STEP
SIDE = CHAINS * HALF


def column_pair(tile):
    return (tile, tile + 8) if tile < 8 else (tile + 8, tile + 12)


def sigmoid(values):
    return 0.5 * jnp.tanh(0.5 * values) + 0.5


def mean_rows(values):
    return jnp.sum(values, axis=0, keepdims=True) * (1.0 / values.shape[0])


def normalize(values):
    center = values - mean_rows(values)
    inverse = lax.rsqrt(mean_rows(center * center) + EPSILON)
    return center * inverse, inverse


def norm_backward(grad_normed, normed, inverse):
    return inverse * (
        grad_normed - mean_rows(grad_normed) - normed * mean_rows(grad_normed * normed)
    )


def dot(first, second, first_dim=1, second_dim=0):
    return lax.dot_general(
        first, second, (((first_dim,), (second_dim,)), ((), ())), preferred_element_type=F32
    )


def swap_halves(values):
    return pltpu.roll(values, HALF, axis=len(values.shape) - 1)


def lower_lanes(shape):
    return lax.broadcasted_iota(jnp.int32, shape, len(shape) - 1) % 128 < HALF


def merge(first, second):
    lower = lower_lanes(first.shape)
    return (
        jnp.where(lower, first, swap_halves(second)),
        jnp.where(lower, swap_halves(first), second),
    )


def kernel(
    x_hbm,
    length_ref,
    ig_ref,
    iw_hbm,
    og_ref,
    ow_hbm,
    ct_hbm,
    out_hbm,
    grad_hbm,
    block,
    iw_ref,
    ow_ref,
    ct_ref,
    flat,
    state,
    upstream,
    mixed,
    norm_in,
    inverse_in,
    norm_out,
    inverse_out,
    projected,
    swap,
    inbox,
    gains,
    weight_t,
    out_weight_t,
    left,
    right,
    grad,
    result,
    send_wide,
    send_slim,
    wide_0,
    wide_1,
    wide_2,
    wide_3,
    slim_0,
    slim_1,
    slim_2,
    slim_3,
    send_sem,
    recv_sem,
    copy_sem,
):
    row, col = lax.axis_index("row"), lax.axis_index("col")
    me = row * COLS + col
    my_chain = col // 2

    loads = [
        pltpu.make_async_copy(source, target, copy_sem.at[i])
        for i, (source, target) in enumerate(
            ((x_hbm, block), (iw_hbm, iw_ref), (ow_hbm, ow_ref), (ct_hbm, ct_ref))
        )
    ]
    for copy in loads:
        copy.start()

    barrier = pltpu.get_barrier_semaphore()

    def greet(t, carry):
        peer = (lax.rem(row + t // COLS, ROWS), lax.rem(col + t % COLS, COLS))
        pl.semaphore_signal(barrier, inc=1, device_id=peer, device_id_type=MESH)
        return carry

    lax.fori_loop(1, DEVICES, greet, 0)

    def send(phase, source, target, chain):
        for step in range(ROWS):
            for part in range(2):
                peer = (lax.rem(row + step, ROWS), chain * 2 + part)
                at = peer[0] * COLS + peer[1]

                def start():
                    pltpu.make_async_remote_copy(
                        source.at[at],
                        target.at[me],
                        send_sem.at[phase],
                        recv_sem.at[phase, my_chain],
                        device_id=peer,
                        device_id_type=MESH,
                    ).start()

                if step > 0:
                    start()
                else:

                    @pl.when(at != me)
                    def _():
                        start()

                    @pl.when(at == me)
                    def _():
                        target[me] = source[me]

    def send_all(body):
        def one(s, carry):
            body(lax.rem(my_chain + s, CHAINS))
            return carry

        lax.fori_loop(0, CHAINS, one, 0)

    def receive(phase, source, target, body):
        def arrived(count):
            some = pl.ds(0, count)
            return pltpu.make_async_remote_copy(
                source.at[some],
                target.at[some],
                send_sem.at[phase],
                recv_sem.at[phase, my_chain],
                device_id=(row, col),
                device_id_type=MESH,
            )

        def one(s, carry):
            chain = lax.rem(my_chain + CHAINS - s, CHAINS)

            def wait(count):
                some = pl.ds(0, count)
                pltpu.make_async_remote_copy(
                    source.at[some],
                    target.at[some],
                    send_sem.at[phase],
                    recv_sem.at[phase, chain],
                    device_id=(row, col),
                    device_id_type=MESH,
                ).wait_recv()

            @pl.when(s == 0)
            def _():
                wait(2 * ROWS - 1)

            @pl.when(s > 0)
            def _():
                wait(2 * ROWS)

            body(chain)
            return carry

        lax.fori_loop(0, CHAINS, one, 0)
        arrived(DEVICES - 1).wait_send()

    def steps(body):
        def one(s, carry):
            body(s, pl.ds(pl.multiple_of(s * STEP, STEP), STEP))
            return carry

        lax.fori_loop(0, STEPS, one, 0)

    def tiles_of(s):
        pairs = []
        for i in range(2):
            tile = s * 2 + i
            late = tile >= 8
            pairs.append((tile + jnp.where(late, 8, 0), tile + jnp.where(late, 12, 8)))
        return pairs

    def valid(s):
        lane = lax.broadcasted_iota(jnp.int32, (1, STEP), 1) + s * STEP
        tile = lane // 128
        token = lane % HALF
        upper = (lane // HALF) % 2
        column = tile + jnp.where(tile < 8, 8 * upper, 8 + 4 * upper) + (col % 2) * WIDTH
        inside = (token < length_ref[row]) & (column < length_ref[my_chain])
        return jnp.where(inside, 1.0, 0.0)

    def load_block(source, target):
        flat[...] = source[...].astype(F32)
        empty = jnp.zeros((HALF - HEIGHT, CH), F32)
        for tile in range(TILES):
            parts = []
            for column in column_pair(tile):
                parts += [flat[pl.ds(column, HEIGHT, stride=WIDTH), :], empty]
            target[:, tile * 128 : (tile + 1) * 128] = jnp.concatenate(parts, axis=0).T

    def store_block(source, target):
        for tile in range(TILES):
            values = source[:, tile * 128 : (tile + 1) * 128].T
            for half, column in enumerate(column_pair(tile)):
                target[pl.ds(column, HEIGHT, stride=WIDTH), :] = values[
                    half * HALF : half * HALF + HEIGHT
                ]

    def put_wide(s, first, second):
        for i, (one, two) in enumerate(tiles_of(s)):
            at = slice(i * 128, (i + 1) * 128)
            lower, upper = merge(first[:, at], second[:, at])
            swap[pl.ds(one, CH, stride=WIDTH), :] = lower
            swap[pl.ds(two, CH, stride=WIDTH), :] = upper

    def get_wide(s):
        firsts, seconds = [], []
        for one, two in tiles_of(s):
            lower, upper = merge(
                inbox[pl.ds(one, CH, stride=WIDTH), :], inbox[pl.ds(two, CH, stride=WIDTH), :]
            )
            firsts.append(lower)
            seconds.append(upper)
        return jnp.concatenate(firsts, axis=1), jnp.concatenate(seconds, axis=1)

    def put_slim(s, values):
        for i in range(2):
            swap[pl.ds(s * 2 + i, CH, stride=16), :] = values[:, i * 128 : (i + 1) * 128]

    def get_slim(s):
        return jnp.concatenate(
            [inbox[pl.ds(s * 2 + i, CH, stride=16), :] for i in range(2)], axis=1
        )

    def channels_of(chain, rows):
        for device_row in range(ROWS):
            at = device_row * COLS + chain * 2
            yield pl.ds(at, 2), pl.ds(pl.multiple_of(at * rows, 2 * rows), 2 * rows)

    def send_swap(phase, source, target, rows):
        def body(chain):
            for messages, at in channels_of(chain, rows):
                source[messages] = swap[at, :].astype(BF16).reshape(2, rows, 128)
            send(phase, source, target, chain)

        send_all(body)

    def receive_swap(phase, source, target, rows):
        def body(chain):
            for messages, at in channels_of(chain, rows):
                inbox[at, :] = target[messages].astype(F32).reshape(2 * rows, 128)

        receive(phase, source, target, body)

    def project(u, s, at, values):
        normed, inverse = normalize(values)
        norm_in[u, :, at] = normed
        inverse_in[u, :, at] = inverse
        mix = dot(weight_t[u], (normed * gains[u]).astype(BF16))
        mixed[u, :, at] = mix
        keep = valid(s)
        put_wide(
            s,
            sigmoid(mix[CH : 2 * CH]) * mix[0:CH] * keep,
            sigmoid(mix[3 * CH : 4 * CH]) * mix[2 * CH : 3 * CH] * keep,
        )

    def finish(u, s, at):
        normed, inverse = normalize(get_slim(s))
        norm_out[u, :, at] = normed
        inverse_out[u, :, at] = inverse
        values = dot(out_weight_t[u], (normed * gains[2 + u]).astype(BF16))
        projected[u, :, at] = values
        gate = sigmoid(mixed[u, 4 * CH :, at])
        after = (state[:, at] + gate * values).astype(BF16).astype(F32)
        state[:, at] = after
        return after, normed, inverse, values, gate

    def finish_back(u, s, at, up, normed, inverse, values, gate):
        grad_projected = up * gate
        mixed[u, 4 * CH :, at] = grad_projected * values * (1.0 - gate)
        grad_scaled = dot(ow_ref[u], grad_projected.astype(BF16))
        put_slim(s, norm_backward(grad_scaled * gains[2 + u], normed, inverse))

    def project_back(u, s, at):
        keep = valid(s)
        parts = []
        for values, base in zip(get_wide(s), (0, 2 * CH)):
            gate = sigmoid(mixed[u, base + CH : base + 2 * CH, at])
            direct = values * gate * keep
            parts.append(direct.astype(BF16))
            parts.append((direct * mixed[u, base : base + CH, at] * (1.0 - gate)).astype(BF16))
        parts.append(mixed[u, 4 * CH :, at].astype(BF16))
        grad_scaled = dot(iw_ref[u], jnp.concatenate(parts, axis=0))
        after = upstream[:, at] + norm_backward(
            grad_scaled * gains[u], norm_in[u, :, at], inverse_in[u, :, at]
        )
        upstream[:, at] = after
        return after

    def places(chain):
        down = pl.ds(pl.multiple_of(chain * HALF, HALF), HALF)
        for pair in range(ROWS // 2):
            indices = [pair * 2 * COLS + chain * 2 + part for part in range(2)]
            yield down, slice(pair * 128, (pair + 1) * 128), indices

    empty = jnp.zeros((HALF - 2 * WIDTH, 128), F32)

    def assemble_wide(phase, source, first, second):
        def body(chain):
            for down, across, indices in places(chain):
                firsts, seconds = [], []
                for at in indices:
                    one, two = merge(source[at].astype(F32), source[at + COLS].astype(F32))
                    firsts.append(one)
                    seconds.append(two)
                first[down, across] = jnp.concatenate(firsts + [empty], axis=0).astype(BF16)
                second[down, across] = jnp.concatenate(seconds + [empty], axis=0).astype(BF16)

        receive(phase, send_wide, source, body)

    def assemble_slim(phase, source, target):
        def body(chain):
            low = lax.broadcasted_iota(jnp.int32, (8, 128), 0) < 4
            for down, across, indices in places(chain):
                parts = []
                for at in indices:
                    one, two = merge(source[at].astype(F32), source[at + COLS].astype(F32))
                    last = jnp.where(low, one[8:16], pltpu.roll(two[8:16], 4, axis=0))
                    parts += [one[0:8], two[0:8], last]
                target[down, across] = jnp.concatenate(parts + [empty], axis=0).astype(BF16)

        receive(phase, send_slim, source, body)

    def split_wide(phase, first, second, target):
        def body(chain):
            for down, across, indices in places(chain):
                lower, upper = merge(first[down, across], second[down, across])
                for part, at in enumerate(indices):
                    cut = slice(part * WIDTH, (part + 1) * WIDTH)
                    send_wide[at] = lower[cut].astype(BF16)
                    send_wide[at + COLS] = upper[cut].astype(BF16)
            send(phase, send_wide, target, chain)

        send_all(body)

    def split_slim(phase, source, target):
        def body(chain):
            for down, across, indices in places(chain):
                values = source[down, across]
                for part, at in enumerate(indices):
                    cut = values[part * WIDTH : (part + 1) * WIDTH]
                    last = cut[16:24]
                    low_0, low_1 = merge(cut[0:8], cut[8:16])
                    high_0, high_1 = merge(last, pltpu.roll(last, 4, axis=0))
                    send_slim[at] = jnp.concatenate([low_0, high_0], axis=0).astype(BF16)
                    send_slim[at + COLS] = jnp.concatenate([low_1, high_1], axis=0).astype(BF16)
            send(phase, send_slim, target, chain)

        send_all(body)

    loads[0].wait()
    load_block(block, state)
    loads[1].wait()
    loads[2].wait()
    for u in range(2):
        weight_t[u] = iw_ref[u].astype(F32).T.astype(BF16)
        out_weight_t[u] = ow_ref[u].astype(F32).T.astype(BF16)
        for i, ref in ((u, ig_ref), (2 + u, og_ref)):
            spread = jnp.broadcast_to(ref[u : u + 1, :], (CH, CH)).T
            gains[i] = jnp.concatenate([spread, spread], axis=1)

    steps(lambda s, at: project(0, s, at, state[:, at]))
    pl.semaphore_wait(barrier, DEVICES - 1)
    send_swap(0, send_wide, wide_0, WIDTH)
    loads[3].wait()
    load_block(ct_ref, upstream)
    assemble_wide(0, wide_0, left.at[0], right.at[0])
    result[0] = dot(right[0], left[0], 0, 0)
    split_slim(1, result.at[0], slim_0)
    receive_swap(1, send_slim, slim_0, 16)

    def middle(s, at):
        project(1, s, at, finish(0, s, at)[0])

    steps(middle)
    send_swap(2, send_wide, wide_1, WIDTH)
    assemble_wide(2, wide_1, left.at[1], right.at[1])
    result[0] = dot(right[1], left[1], 1, 1)
    split_slim(3, result.at[0], slim_1)
    receive_swap(3, send_slim, slim_1, 16)

    def top(s, at):
        _, normed, inverse, values, gate = finish(1, s, at)
        finish_back(1, s, at, upstream[:, at], normed, inverse, values, gate)

    steps(top)
    send_swap(4, send_slim, slim_2, 16)
    store_block(state, flat)
    block[...] = flat[...].astype(BF16)
    store = pltpu.make_async_copy(block, out_hbm, copy_sem.at[0])
    store.start()
    assemble_slim(4, slim_2, grad)
    result[0] = dot(grad[...], right[1], 0, 0)
    result[1] = dot(grad[...], left[1], 1, 0)
    split_wide(5, result.at[0], result.at[1], wide_2)
    receive_swap(5, send_wide, wide_2, WIDTH)

    steps(lambda s, at: project_back(1, s, at))

    def bottom(s, at):
        gate = sigmoid(mixed[0, 4 * CH :, at])
        finish_back(
            0,
            s,
            at,
            upstream[:, at],
            norm_out[0, :, at],
            inverse_out[0, :, at],
            projected[0, :, at],
            gate,
        )

    steps(bottom)
    send_swap(6, send_slim, slim_3, 16)
    assemble_slim(6, slim_3, grad)
    result[0] = dot(right[0], grad[...], 1, 0)
    result[1] = dot(left[0], grad[...], 1, 1)
    split_wide(7, result.at[0], result.at[1], wide_3)
    receive_swap(7, send_wide, wide_3, WIDTH)

    steps(lambda s, at: project_back(0, s, at))
    store_block(upstream, flat)
    final = pltpu.make_async_copy(flat, grad_hbm, copy_sem.at[1])
    final.start()
    store.wait()
    final.wait()


def local(
    pair_input, chain_lengths, input_gain, input_weight, output_gain, output_weight, cotangent
):
    cells = HEIGHT * WIDTH
    vmem = pl.BlockSpec(memory_space=pltpu.VMEM)
    hbm = pl.BlockSpec(memory_space=pl.ANY)
    smem = pl.BlockSpec(memory_space=pltpu.SMEM)
    wide = pltpu.VMEM((DEVICES, WIDTH, 128), BF16)
    slim = pltpu.VMEM((DEVICES, 16, 128), BF16)
    plane = pltpu.VMEM((CH, LANES), F32)
    planes = pltpu.VMEM((2, CH, LANES), F32)
    line = pltpu.VMEM((2, 1, LANES), F32)
    out, grad = pl.pallas_call(
        kernel,
        out_shape=(
            jax.ShapeDtypeStruct((cells, CH), BF16),
            jax.ShapeDtypeStruct((cells, CH), F32),
        ),
        in_specs=[hbm, smem, vmem, hbm, vmem, hbm, hbm],
        out_specs=(hbm, hbm),
        scratch_shapes=[
            pltpu.VMEM((cells, CH), BF16),
            pltpu.VMEM((2, CH, 5 * CH), BF16),
            pltpu.VMEM((2, CH, CH), BF16),
            pltpu.VMEM((cells, CH), BF16),
            pltpu.VMEM((cells, CH), F32),
            plane,
            plane,
            pltpu.VMEM((2, 5 * CH, LANES), F32),
            planes,
            line,
            planes,
            line,
            planes,
            pltpu.VMEM((CH * WIDTH, 128), F32),
            pltpu.VMEM((CH * WIDTH, 128), F32),
            pltpu.VMEM((4, CH, STEP), F32),
            pltpu.VMEM((2, 5 * CH, CH), BF16),
            pltpu.VMEM((2, CH, CH), BF16),
            pltpu.VMEM((2, SIDE, SIDE), BF16),
            pltpu.VMEM((2, SIDE, SIDE), BF16),
            pltpu.VMEM((SIDE, SIDE), BF16),
            pltpu.VMEM((2, SIDE, SIDE), F32),
            wide,
            slim,
            wide,
            wide,
            wide,
            wide,
            slim,
            slim,
            slim,
            slim,
            pltpu.SemaphoreType.DMA((8,)),
            pltpu.SemaphoreType.DMA((8, CHAINS)),
            pltpu.SemaphoreType.DMA((4,)),
        ],
        compiler_params=pltpu.CompilerParams(
            collective_id=0, has_side_effects=True, vmem_limit_bytes=52 * 2**20
        ),
    )(
        pair_input.reshape(cells, CH),
        chain_lengths,
        input_gain,
        input_weight,
        output_gain,
        output_weight,
        cotangent.reshape(cells, CH),
    )
    shape = (HEIGHT, WIDTH, CH)
    return out.reshape(shape), grad.reshape(shape)


def solution(mesh):
    placed = (P("row", "col", None), P(), P(), P(), P(), P(), P("row", "col", None))
    return jax.shard_map(
        local,
        mesh=mesh,
        in_specs=placed,
        out_specs=(P("row", "col", None), P("row", "col", None)),
        check_vma=False,
    )
```

```python
import functools

import jax
import jax.numpy as jnp
from jax import lax
from jax.experimental import pallas as pl
from jax.experimental.pallas import tpu as pltpu
from jax.sharding import PartitionSpec as P

MESH = pl.DeviceIdType.MESH
F32 = jnp.float32
BF16 = jnp.bfloat16

CH = 128
N = 384
CHAINS = 8
EPSILON = 1e-05

ROWS, COLS = 8, 16
DEVICES = ROWS * COLS
HEIGHT, WIDTH = N // ROWS, N // COLS
HALF = 64
TILES = WIDTH // 2
LANES = TILES * 128
STEP = 256
STEPS = LANES // STEP
SIDE = CHAINS * HALF


def column_pair(tile):
    return (tile, tile + 8) if tile < 8 else (tile + 8, tile + 12)


def sigmoid(values):
    return 0.5 * jnp.tanh(0.5 * values) + 0.5


def mean_rows(values):
    return jnp.sum(values, axis=0, keepdims=True) * (1.0 / values.shape[0])


def normalize(values):
    center = values - mean_rows(values)
    inverse = lax.rsqrt(mean_rows(center * center) + EPSILON)
    return center * inverse, inverse


def norm_backward(grad_normed, normed, inverse):
    return inverse * (
        grad_normed - mean_rows(grad_normed) - normed * mean_rows(grad_normed * normed)
    )


def dot(first, second, first_dim=1, second_dim=0):
    return lax.dot_general(
        first, second, (((first_dim,), (second_dim,)), ((), ())), preferred_element_type=F32
    )


def swap_halves(values):
    return pltpu.roll(values, HALF, axis=len(values.shape) - 1)


def lower_lanes(shape):
    return lax.broadcasted_iota(jnp.int32, shape, len(shape) - 1) % 128 < HALF


def merge(first, second):
    lower = lower_lanes(first.shape)
    return (
        jnp.where(lower, first, swap_halves(second)),
        jnp.where(lower, swap_halves(first), second),
    )


def kernel(
    x_hbm,
    length_ref,
    ig_ref,
    iw_hbm,
    og_ref,
    ow_hbm,
    ct_hbm,
    out_hbm,
    grad_hbm,
    block,
    iw_ref,
    ow_ref,
    ct_ref,
    flat,
    state,
    upstream,
    mixed,
    norm_in,
    inverse_in,
    norm_out,
    inverse_out,
    projected,
    swap,
    inbox,
    gains,
    weight_t,
    out_weight_t,
    left,
    right,
    grad,
    result,
    send_wide,
    send_slim,
    wide_0,
    wide_1,
    wide_2,
    wide_3,
    slim_0,
    slim_1,
    slim_2,
    slim_3,
    send_sem,
    recv_sem,
    copy_sem,
):
    row, col = lax.axis_index("row"), lax.axis_index("col")
    me = row * COLS + col
    my_chain = col // 2
    my_pair = row // 2
    my_group = lax.rem(my_chain + 2 * (4 - my_pair), CHAINS)

    loads = [
        pltpu.make_async_copy(source, target, copy_sem.at[i])
        for i, (source, target) in enumerate(
            ((x_hbm, block), (iw_hbm, iw_ref), (ow_hbm, ow_ref), (ct_hbm, ct_ref))
        )
    ]
    for copy in loads:
        copy.start()

    barrier = pltpu.get_barrier_semaphore()

    def greet(t, carry):
        peer = (lax.rem(row + t // COLS, ROWS), lax.rem(col + t % COLS, COLS))
        pl.semaphore_signal(barrier, inc=1, device_id=peer, device_id_type=MESH)
        return carry

    lax.fori_loop(1, DEVICES, greet, 0)

    def chain_of(group, pair):
        return lax.rem(group + 2 * pair, CHAINS)

    def send(phase, source, target, group):
        for step in range(ROWS // 2):
            pair = lax.rem(my_pair + step, ROWS // 2)
            chain = chain_of(group, pair)
            for low in range(2):
                for part in range(2):
                    peer = (pair * 2 + lax.rem(row + low, 2), chain * 2 + part)
                    at = peer[0] * COLS + peer[1]

                    def start(peer=peer, at=at):
                        pltpu.make_async_remote_copy(
                            source.at[at],
                            target.at[me],
                            send_sem.at[phase],
                            recv_sem.at[phase, my_group],
                            device_id=peer,
                            device_id_type=MESH,
                        ).start()

                    if step + low > 0:
                        start()
                    else:

                        @pl.when(at != me)
                        def _():
                            start()

                        @pl.when(at == me)
                        def _():
                            target[me] = source[me]

    def send_all(body):
        def one(s, carry):
            body(lax.rem(my_group + s, CHAINS))
            return carry

        lax.fori_loop(0, CHAINS, one, 0)

    def receive(phase, source, target, body):
        def arrived(count):
            some = pl.ds(0, count)
            return pltpu.make_async_remote_copy(
                source.at[some],
                target.at[some],
                send_sem.at[phase],
                recv_sem.at[phase, my_group],
                device_id=(row, col),
                device_id_type=MESH,
            )

        def one(s, carry):
            group = lax.rem(my_group + CHAINS - s, CHAINS)

            def wait(count):
                some = pl.ds(0, count)
                pltpu.make_async_remote_copy(
                    source.at[some],
                    target.at[some],
                    send_sem.at[phase],
                    recv_sem.at[phase, group],
                    device_id=(row, col),
                    device_id_type=MESH,
                ).wait_recv()

            @pl.when(s == 0)
            def _():
                wait(2 * ROWS - 1)

            @pl.when(s > 0)
            def _():
                wait(2 * ROWS)

            body(group)
            return carry

        lax.fori_loop(0, CHAINS, one, 0)
        arrived(DEVICES - 1).wait_send()

    def steps(body):
        def one(s, carry):
            body(s, pl.ds(pl.multiple_of(s * STEP, STEP), STEP))
            return carry

        lax.fori_loop(0, STEPS, one, 0, unroll=True)

    def tiles_of(s):
        pairs = []
        for i in range(2):
            tile = s * 2 + i
            late = tile >= 8
            pairs.append((tile + jnp.where(late, 8, 0), tile + jnp.where(late, 12, 8)))
        return pairs

    def valid(s):
        lane = lax.broadcasted_iota(jnp.int32, (1, STEP), 1) + s * STEP
        tile = lane // 128
        token = lane % HALF
        upper = (lane // HALF) % 2
        column = tile + jnp.where(tile < 8, 8 * upper, 8 + 4 * upper) + (col % 2) * WIDTH
        inside = (token < length_ref[row]) & (column < length_ref[my_chain])
        return jnp.where(inside, 1.0, 0.0)

    def load_block(source, target):
        flat[...] = source[...].astype(F32)
        empty = jnp.zeros((HALF - HEIGHT, CH), F32)
        for tile in range(TILES):
            parts = []
            for column in column_pair(tile):
                parts += [flat[pl.ds(column, HEIGHT, stride=WIDTH), :], empty]
            target[:, tile * 128 : (tile + 1) * 128] = jnp.concatenate(parts, axis=0).T

    def store_block(source, target):
        for tile in range(TILES):
            values = source[:, tile * 128 : (tile + 1) * 128].T
            for half, column in enumerate(column_pair(tile)):
                target[pl.ds(column, HEIGHT, stride=WIDTH), :] = values[
                    half * HALF : half * HALF + HEIGHT
                ]

    def put_wide(s, first, second):
        for i, (one, two) in enumerate(tiles_of(s)):
            at = slice(i * 128, (i + 1) * 128)
            lower, upper = merge(first[:, at], second[:, at])
            swap[pl.ds(one, CH, stride=WIDTH), :] = lower
            swap[pl.ds(two, CH, stride=WIDTH), :] = upper

    def get_wide(s):
        firsts, seconds = [], []
        for one, two in tiles_of(s):
            lower, upper = merge(
                inbox[pl.ds(one, CH, stride=WIDTH), :], inbox[pl.ds(two, CH, stride=WIDTH), :]
            )
            firsts.append(lower)
            seconds.append(upper)
        return jnp.concatenate(firsts, axis=1), jnp.concatenate(seconds, axis=1)

    def put_slim(s, values):
        for i in range(2):
            swap[pl.ds(s * 2 + i, CH, stride=TILES), :] = values[:, i * 128 : (i + 1) * 128]

    def get_slim(s):
        return jnp.concatenate(
            [inbox[pl.ds(s * 2 + i, CH, stride=TILES), :] for i in range(2)], axis=1
        )

    def channels_of(group, rows):
        for device_row in range(ROWS):
            at = device_row * COLS + chain_of(group, device_row // 2) * 2
            yield pl.ds(at, 2), pl.ds(pl.multiple_of(at * rows, 2 * rows), 2 * rows)

    def send_swap(phase, source, target, rows):
        def body(group):
            for messages, at in channels_of(group, rows):
                source[messages] = swap[at, :].astype(BF16).reshape((2,) + source.shape[1:])
            send(phase, source, target, group)

        send_all(body)

    def receive_swap(phase, source, target, rows):
        def body(group):
            for messages, at in channels_of(group, rows):
                inbox[at, :] = target[messages].astype(F32).reshape(2 * rows, 128)

        receive(phase, source, target, body)

    def project(u, s, at, values):
        normed, inverse = normalize(values)
        norm_in[u, :, at] = normed
        inverse_in[u, :, at] = inverse
        mix = dot(weight_t[u], (normed * gains[u]).astype(BF16))
        mixed[u, :, at] = mix
        keep = valid(s)
        put_wide(
            s,
            sigmoid(mix[CH : 2 * CH]) * mix[0:CH] * keep,
            sigmoid(mix[3 * CH : 4 * CH]) * mix[2 * CH : 3 * CH] * keep,
        )

    def finish(u, s, at):
        normed, inverse = normalize(get_slim(s))
        norm_out[u, :, at] = normed
        inverse_out[u, :, at] = inverse
        values = dot(out_weight_t[u], (normed * gains[2 + u]).astype(BF16))
        projected[u, :, at] = values
        gate = sigmoid(mixed[u, 4 * CH :, at])
        after = (state[:, at] + gate * values).astype(BF16).astype(F32)
        state[:, at] = after
        return after, normed, inverse, values, gate

    def finish_back(u, s, at, up, normed, inverse, values, gate):
        grad_projected = up * gate
        mixed[u, 4 * CH :, at] = grad_projected * values * (1.0 - gate)
        grad_scaled = dot(ow_ref[u], grad_projected.astype(BF16))
        put_slim(s, norm_backward(grad_scaled * gains[2 + u], normed, inverse))

    def project_back(u, s, at):
        keep = valid(s)
        parts = []
        for values, base in zip(get_wide(s), (0, 2 * CH)):
            gate = sigmoid(mixed[u, base + CH : base + 2 * CH, at])
            direct = values * gate * keep
            parts.append(direct.astype(BF16))
            parts.append((direct * mixed[u, base : base + CH, at] * (1.0 - gate)).astype(BF16))
        parts.append(mixed[u, 4 * CH :, at].astype(BF16))
        grad_scaled = dot(iw_ref[u], jnp.concatenate(parts, axis=0))
        after = upstream[:, at] + norm_backward(
            grad_scaled * gains[u], norm_in[u, :, at], inverse_in[u, :, at]
        )
        upstream[:, at] = after
        return after

    def places(group):
        for pair in range(ROWS // 2):
            chain = chain_of(group, pair)
            down = pl.ds(pl.multiple_of(chain * HALF, HALF), HALF)
            indices = [pair * 2 * COLS + chain * 2 + part for part in range(2)]
            yield down, slice(pair * 128, (pair + 1) * 128), indices

    empty = jnp.zeros((HALF - 2 * WIDTH, 128), F32)

    def assemble_wide(phase, source, first, second):
        def body(group):
            for down, across, indices in places(group):
                firsts, seconds = [], []
                for at in indices:
                    one, two = merge(source[at].astype(F32), source[at + COLS].astype(F32))
                    firsts.append(one)
                    seconds.append(two)
                first[down, across] = jnp.concatenate(firsts + [empty], axis=0).astype(BF16)
                second[down, across] = jnp.concatenate(seconds + [empty], axis=0).astype(BF16)

        receive(phase, send_wide, source, body)

    def open_slim(source, at):
        rows = source[at].astype(F32).reshape(TILES, 128)
        return jnp.concatenate([rows, jnp.zeros((4, 128), F32)], axis=0)

    def assemble_slim(phase, source, target):
        def body(group):
            low = lax.broadcasted_iota(jnp.int32, (8, 128), 0) < 4
            for down, across, indices in places(group):
                parts = []
                for at in indices:
                    one, two = merge(open_slim(source, at), open_slim(source, at + COLS))
                    last = jnp.where(low, one[8:16], pltpu.roll(two[8:16], 4, axis=0))
                    parts += [one[0:8], two[0:8], last]
                target[down, across] = jnp.concatenate(parts + [empty], axis=0).astype(BF16)

        receive(phase, send_slim, source, body)

    def split_wide(phase, first, second, target):
        def body(group):
            for down, across, indices in places(group):
                lower, upper = merge(first[down, across], second[down, across])
                for part, at in enumerate(indices):
                    cut = slice(part * WIDTH, (part + 1) * WIDTH)
                    send_wide[at] = lower[cut].astype(BF16)
                    send_wide[at + COLS] = upper[cut].astype(BF16)
            send(phase, send_wide, target, group)

        send_all(body)

    def split_slim(phase, source, target):
        def body(group):
            for down, across, indices in places(group):
                values = source[down, across]
                for part, at in enumerate(indices):
                    cut = values[part * WIDTH : (part + 1) * WIDTH]
                    last = cut[16:24]
                    low_0, low_1 = merge(cut[0:8], cut[8:16])
                    high_0, high_1 = merge(last, pltpu.roll(last, 4, axis=0))
                    for to, lines in ((at, (low_0, high_0)), (at + COLS, (low_1, high_1))):
                        rows = jnp.concatenate([lines[0], lines[1][0:4]], axis=0)
                        send_slim[to] = rows.astype(BF16).reshape(3, 4, 128)
            send(phase, send_slim, target, group)

        send_all(body)

    loads[0].wait()
    load_block(block, state)
    loads[1].wait()
    loads[2].wait()
    for u in range(2):
        weight_t[u] = iw_ref[u].astype(F32).T.astype(BF16)
        out_weight_t[u] = ow_ref[u].astype(F32).T.astype(BF16)
        for i, ref in ((u, ig_ref), (2 + u, og_ref)):
            spread = jnp.broadcast_to(ref[u : u + 1, :], (CH, CH)).T
            gains[i] = jnp.concatenate([spread, spread], axis=1)

    steps(lambda s, at: project(0, s, at, state[:, at]))
    pl.semaphore_wait(barrier, DEVICES - 1)
    send_swap(0, send_wide, wide_0, WIDTH)
    loads[3].wait()
    load_block(ct_ref, upstream)
    assemble_wide(0, wide_0, left.at[0], right.at[0])
    result[0] = dot(right[0], left[0], 0, 0)
    split_slim(1, result.at[0], slim_0)
    receive_swap(1, send_slim, slim_0, TILES)

    def middle(s, at):
        project(1, s, at, finish(0, s, at)[0])

    steps(middle)
    send_swap(2, send_wide, wide_1, WIDTH)
    assemble_wide(2, wide_1, left.at[1], right.at[1])
    result[0] = dot(right[1], left[1], 1, 1)
    split_slim(3, result.at[0], slim_1)
    receive_swap(3, send_slim, slim_1, TILES)

    def top(s, at):
        _, normed, inverse, values, gate = finish(1, s, at)
        finish_back(1, s, at, upstream[:, at], normed, inverse, values, gate)

    steps(top)
    send_swap(4, send_slim, slim_2, TILES)
    store_block(state, flat)
    block[...] = flat[...].astype(BF16)
    store = pltpu.make_async_copy(block, out_hbm, copy_sem.at[0])
    store.start()
    assemble_slim(4, slim_2, grad)
    result[0] = dot(grad[...], right[1], 0, 0)
    result[1] = dot(grad[...], left[1], 1, 0)
    split_wide(5, result.at[0], result.at[1], wide_2)
    receive_swap(5, send_wide, wide_2, WIDTH)

    steps(lambda s, at: project_back(1, s, at))

    def bottom(s, at):
        gate = sigmoid(mixed[0, 4 * CH :, at])
        finish_back(
            0,
            s,
            at,
            upstream[:, at],
            norm_out[0, :, at],
            inverse_out[0, :, at],
            projected[0, :, at],
            gate,
        )

    steps(bottom)
    send_swap(6, send_slim, slim_3, TILES)
    assemble_slim(6, slim_3, grad)
    result[0] = dot(right[0], grad[...], 1, 0)
    result[1] = dot(left[0], grad[...], 1, 1)
    split_wide(7, result.at[0], result.at[1], wide_3)
    receive_swap(7, send_wide, wide_3, WIDTH)

    steps(lambda s, at: project_back(0, s, at))
    store_block(upstream, flat)
    final = pltpu.make_async_copy(flat, grad_hbm, copy_sem.at[1])
    final.start()
    store.wait()
    final.wait()


def local(
    pair_input, chain_lengths, input_gain, input_weight, output_gain, output_weight, cotangent
):
    cells = HEIGHT * WIDTH
    vmem = pl.BlockSpec(memory_space=pltpu.VMEM)
    hbm = pl.BlockSpec(memory_space=pl.ANY)
    smem = pl.BlockSpec(memory_space=pltpu.SMEM)
    wide = pltpu.VMEM((DEVICES, WIDTH, 128), BF16)
    slim = pltpu.VMEM((DEVICES, 3, 4, 128), BF16)
    plane = pltpu.VMEM((CH, LANES), F32)
    planes = pltpu.VMEM((2, CH, LANES), F32)
    line = pltpu.VMEM((2, 1, LANES), F32)
    out, grad = pl.pallas_call(
        kernel,
        out_shape=(
            jax.ShapeDtypeStruct((cells, CH), BF16),
            jax.ShapeDtypeStruct((cells, CH), F32),
        ),
        in_specs=[hbm, smem, vmem, hbm, vmem, hbm, hbm],
        out_specs=(hbm, hbm),
        scratch_shapes=[
            pltpu.VMEM((cells, CH), BF16),
            pltpu.VMEM((2, CH, 5 * CH), BF16),
            pltpu.VMEM((2, CH, CH), BF16),
            pltpu.VMEM((cells, CH), BF16),
            pltpu.VMEM((cells, CH), F32),
            plane,
            plane,
            pltpu.VMEM((2, 5 * CH, LANES), F32),
            planes,
            line,
            planes,
            line,
            planes,
            pltpu.VMEM((CH * WIDTH, 128), F32),
            pltpu.VMEM((CH * WIDTH, 128), F32),
            pltpu.VMEM((4, CH, STEP), F32),
            pltpu.VMEM((2, 5 * CH, CH), BF16),
            pltpu.VMEM((2, CH, CH), BF16),
            pltpu.VMEM((2, SIDE, SIDE), BF16),
            pltpu.VMEM((2, SIDE, SIDE), BF16),
            pltpu.VMEM((SIDE, SIDE), BF16),
            pltpu.VMEM((2, SIDE, SIDE), F32),
            wide,
            slim,
            wide,
            wide,
            wide,
            wide,
            slim,
            slim,
            slim,
            slim,
            pltpu.SemaphoreType.DMA((8,)),
            pltpu.SemaphoreType.DMA((8, CHAINS)),
            pltpu.SemaphoreType.DMA((4,)),
        ],
        compiler_params=pltpu.CompilerParams(
            collective_id=0, has_side_effects=True, vmem_limit_bytes=52 * 2**20
        ),
    )(
        pair_input.reshape(cells, CH),
        chain_lengths,
        input_gain,
        input_weight,
        output_gain,
        output_weight,
        cotangent.reshape(cells, CH),
    )
    shape = (HEIGHT, WIDTH, CH)
    return out.reshape(shape), grad.reshape(shape)


def solution(mesh):
    placed = (P("row", "col", None), P(), P(), P(), P(), P(), P("row", "col", None))
    return jax.shard_map(
        local,
        mesh=mesh,
        in_specs=placed,
        out_specs=(P("row", "col", None), P("row", "col", None)),
        check_vma=False,
    )
```

```python
import functools

import jax
import jax.numpy as jnp
from jax import lax
from jax.experimental import pallas as pl
from jax.experimental.pallas import tpu as pltpu
from jax.sharding import PartitionSpec as P

MESH = pl.DeviceIdType.MESH
F32 = jnp.float32
BF16 = jnp.bfloat16

CH = 128
N = 384
CHAINS = 8
EPSILON = 1e-05

ROWS, COLS = 8, 16
DEVICES = ROWS * COLS
HEIGHT, WIDTH = N // ROWS, N // COLS
HALF = 64
TILES = WIDTH // 2
LANES = TILES * 128
STEP = 256
STEPS = LANES // STEP
SIDE = CHAINS * HALF


UNITS = (
    (20842, 2390, 4165),
    (64490, 1022, 4164),
    (325, 6122, 17489),
    (1007, 15690, 1105),
)


def column_pair(tile):
    return (tile, tile + 8) if tile < 8 else (tile + 8, tile + 12)


def sigmoid(values):
    return 0.5 * jnp.tanh(0.5 * values) + 0.5


def mean_rows(values):
    return jnp.sum(values, axis=0, keepdims=True) * (1.0 / values.shape[0])


def normalize(values):
    center = values - mean_rows(values)
    inverse = lax.rsqrt(mean_rows(center * center) + EPSILON)
    return center * inverse, inverse


def norm_backward(grad_normed, normed, inverse):
    return inverse * (
        grad_normed - mean_rows(grad_normed) - normed * mean_rows(grad_normed * normed)
    )


def dot(first, second, first_dim=1, second_dim=0):
    return lax.dot_general(
        first, second, (((first_dim,), (second_dim,)), ((), ())), preferred_element_type=F32
    )


def swap_halves(values):
    return pltpu.roll(values, HALF, axis=len(values.shape) - 1)


def lower_lanes(shape):
    return lax.broadcasted_iota(jnp.int32, shape, len(shape) - 1) % 128 < HALF


def merge(first, second):
    lower = lower_lanes(first.shape)
    return (
        jnp.where(lower, first, swap_halves(second)),
        jnp.where(lower, swap_halves(first), second),
    )


def kernel(
    x_hbm,
    length_ref,
    ig_ref,
    iw_hbm,
    og_ref,
    ow_hbm,
    ct_hbm,
    out_hbm,
    grad_hbm,
    block,
    iw_ref,
    ow_ref,
    ct_ref,
    flat,
    state,
    upstream,
    mixed,
    norm_in,
    inverse_in,
    norm_out,
    inverse_out,
    projected,
    early_back,
    swap,
    inbox,
    gains,
    weight_t,
    out_weight_t,
    left,
    right,
    grad,
    result,
    send_wide,
    send_slim,
    wide_0,
    wide_1,
    wide_2,
    wide_3,
    slim_0,
    slim_1,
    slim_2,
    slim_3,
    send_sem,
    recv_sem,
    copy_sem,
):
    row, col = lax.axis_index("row"), lax.axis_index("col")
    me = row * COLS + col
    my_chain = col // 2
    my_pair = row // 2

    loads = [
        pltpu.make_async_copy(source, target, copy_sem.at[i])
        for i, (source, target) in enumerate(
            ((x_hbm, block), (iw_hbm, iw_ref), (ow_hbm, ow_ref), (ct_hbm, ct_ref))
        )
    ]
    for copy in loads:
        copy.start()

    barrier = pltpu.get_barrier_semaphore()

    def greet(first, last):
        for t in range(first, last):
            peer = (lax.rem(row + t // COLS, ROWS), lax.rem(col + t % COLS, COLS))
            pl.semaphore_signal(barrier, inc=1, device_id=peer, device_id_type=MESH)

    def units_of(group, sign):
        for offsets in UNITS:
            x, z, y = [(bits >> (2 * group)) & 3 for bits in offsets]
            pair = (my_pair + sign * z) & 3
            chain = ((my_chain // 2 + sign * x) & 3) * 2 + (my_chain + y) % 2
            yield pair, chain

    def send(phase, source, target, group):
        for unit, (pair, chain) in enumerate(units_of(group, 1)):
            for low in range(2):
                for part in range(2):
                    peer = (pair * 2 + lax.rem(row + low, 2), chain * 2 + part)
                    at = peer[0] * COLS + peer[1]

                    def start(peer=peer, at=at):
                        pltpu.make_async_remote_copy(
                            source.at[at],
                            target.at[me],
                            send_sem.at[phase],
                            recv_sem.at[phase, group],
                            device_id=peer,
                            device_id_type=MESH,
                        ).start()

                    if unit < 3 or low > 0:
                        start()
                    else:

                        @pl.when(at != me)
                        def _():
                            start()

                        @pl.when(at == me)
                        def _():
                            target[me] = source[me]

    def send_all(body):
        def one(s, carry):
            body(s)
            return carry

        lax.fori_loop(0, CHAINS, one, 0)

    def receive(phase, source, target, body):
        def arrived(count):
            some = pl.ds(0, count)
            return pltpu.make_async_remote_copy(
                source.at[some],
                target.at[some],
                send_sem.at[phase],
                recv_sem.at[phase, 0],
                device_id=(row, col),
                device_id_type=MESH,
            )

        def one(group, carry):
            def wait(count):
                some = pl.ds(0, count)
                pltpu.make_async_remote_copy(
                    source.at[some],
                    target.at[some],
                    send_sem.at[phase],
                    recv_sem.at[phase, group],
                    device_id=(row, col),
                    device_id_type=MESH,
                ).wait_recv()

            @pl.when(group == CHAINS - 1)
            def _():
                wait(2 * ROWS - 1)

            @pl.when(group < CHAINS - 1)
            def _():
                wait(2 * ROWS)

            body(group)
            return carry

        lax.fori_loop(0, CHAINS, one, 0)
        arrived(DEVICES - 1).wait_send()

    def steps(body):
        def one(s, carry):
            body(s, pl.ds(pl.multiple_of(s * STEP, STEP), STEP))
            return carry

        lax.fori_loop(0, STEPS, one, 0, unroll=True)

    def tiles_of(s):
        pairs = []
        for i in range(2):
            tile = s * 2 + i
            late = tile >= 8
            pairs.append((tile + jnp.where(late, 8, 0), tile + jnp.where(late, 12, 8)))
        return pairs

    def valid(s):
        lane = lax.broadcasted_iota(jnp.int32, (1, STEP), 1) + s * STEP
        tile = lane // 128
        token = lane % HALF
        upper = (lane // HALF) % 2
        column = tile + jnp.where(tile < 8, 8 * upper, 8 + 4 * upper) + (col % 2) * WIDTH
        inside = (token < length_ref[row]) & (column < length_ref[my_chain])
        return jnp.where(inside, 1.0, 0.0)

    def load_block(source, target, beside=lambda tile: None):
        flat[...] = source[...].astype(F32)
        empty = jnp.zeros((HALF - HEIGHT, CH), F32)
        for tile in range(TILES):
            parts = []
            for column in column_pair(tile):
                parts += [flat[pl.ds(column, HEIGHT, stride=WIDTH), :], empty]
            target[:, tile * 128 : (tile + 1) * 128] = jnp.concatenate(parts, axis=0).T
            beside(tile)

    def store_block(source, target):
        for tile in range(TILES):
            values = source[:, tile * 128 : (tile + 1) * 128].T
            for half, column in enumerate(column_pair(tile)):
                target[pl.ds(column, HEIGHT, stride=WIDTH), :] = values[
                    half * HALF : half * HALF + HEIGHT
                ]

    def put_wide(s, first, second):
        for i, (one, two) in enumerate(tiles_of(s)):
            at = slice(i * 128, (i + 1) * 128)
            lower, upper = merge(first[:, at], second[:, at])
            swap[pl.ds(one, CH, stride=WIDTH), :] = lower
            swap[pl.ds(two, CH, stride=WIDTH), :] = upper

    def get_wide(s):
        firsts, seconds = [], []
        for one, two in tiles_of(s):
            lower, upper = merge(
                inbox[pl.ds(one, CH, stride=WIDTH), :], inbox[pl.ds(two, CH, stride=WIDTH), :]
            )
            firsts.append(lower)
            seconds.append(upper)
        return jnp.concatenate(firsts, axis=1), jnp.concatenate(seconds, axis=1)

    def put_slim(s, values):
        for i in range(2):
            swap[pl.ds(s * 2 + i, CH, stride=TILES), :] = values[:, i * 128 : (i + 1) * 128]

    def get_slim(s):
        return jnp.concatenate(
            [inbox[pl.ds(s * 2 + i, CH, stride=TILES), :] for i in range(2)], axis=1
        )

    def channels_of(group, sign, rows):
        for pair, chain in units_of(group, sign):
            for low in range(2):
                at = (pair * 2 + low) * COLS + chain * 2
                yield pl.ds(at, 2), pl.ds(pl.multiple_of(at * rows, 2 * rows), 2 * rows)

    def send_swap(phase, source, target, rows):
        def body(group):
            for messages, at in channels_of(group, 1, rows):
                source[messages] = swap[at, :].astype(BF16).reshape((2,) + source.shape[1:])
            send(phase, source, target, group)

        send_all(body)

    def receive_swap(phase, source, target, rows):
        def body(group):
            for messages, at in channels_of(group, -1, rows):
                inbox[at, :] = target[messages].astype(F32).reshape(2 * rows, 128)

        receive(phase, source, target, body)

    def project(u, s, at, values):
        normed, inverse = normalize(values)
        norm_in[u, :, at] = normed
        inverse_in[u, :, at] = inverse
        mix = dot(weight_t[u], (normed * gains[u]).astype(BF16))
        mixed[u, :, at] = mix
        keep = valid(s)
        put_wide(
            s,
            sigmoid(mix[CH : 2 * CH]) * mix[0:CH] * keep,
            sigmoid(mix[3 * CH : 4 * CH]) * mix[2 * CH : 3 * CH] * keep,
        )

    def finish(u, s, at):
        normed, inverse = normalize(get_slim(s))
        norm_out[u, :, at] = normed
        inverse_out[u, :, at] = inverse
        values = dot(out_weight_t[u], (normed * gains[2 + u]).astype(BF16))
        projected[u, :, at] = values
        gate = mixed[u, 4 * CH :, at]
        after = (state[:, at] + gate * values).astype(BF16).astype(F32)
        state[:, at] = after
        return after, normed, inverse, values, gate

    def scaled_back(u, at, grad_projected):
        return dot(ow_ref[u], grad_projected.astype(BF16)) * gains[2 + u]

    def early(s, at):
        early_back[:, at] = scaled_back(1, at, upstream[:, at] * mixed[1, 4 * CH :, at])

    def finish_back(u, s, at, up, normed, inverse, values, gate, grad_scaled=None):
        grad_projected = up * gate
        mixed[u, 4 * CH :, at] = grad_projected * values * (1.0 - gate)
        if grad_scaled is None:
            grad_scaled = scaled_back(u, at, grad_projected)
        put_slim(s, norm_backward(grad_scaled, normed, inverse))

    def gates(u, s, at):
        mixed[u, 4 * CH :, at] = sigmoid(mixed[u, 4 * CH :, at])

    def factors(u, s, at):
        keep = valid(s)
        for base in (0, 2 * CH):
            gate = sigmoid(mixed[u, base + CH : base + 2 * CH, at])
            kept = gate * keep
            mixed[u, base : base + CH, at] = mixed[u, base : base + CH, at] * kept * (1.0 - gate)
            mixed[u, base + CH : base + 2 * CH, at] = kept

    def project_back(u, s, at):
        parts = []
        for values, base in zip(get_wide(s), (0, 2 * CH)):
            parts.append((values * mixed[u, base + CH : base + 2 * CH, at]).astype(BF16))
            parts.append((values * mixed[u, base : base + CH, at]).astype(BF16))
        parts.append(mixed[u, 4 * CH :, at].astype(BF16))
        grad_scaled = dot(iw_ref[u], jnp.concatenate(parts, axis=0))
        after = upstream[:, at] + norm_backward(
            grad_scaled * gains[u], norm_in[u, :, at], inverse_in[u, :, at]
        )
        upstream[:, at] = after
        return after

    def places(group, sign):
        for pair, chain in units_of(group, sign):
            yield (
                pl.ds(pl.multiple_of(chain * HALF, HALF), HALF),
                pl.ds(pl.multiple_of(pair * 128, 128), 128),
                [pair * 2 * COLS + chain * 2 + part for part in range(2)],
            )

    empty = jnp.zeros((HALF - 2 * WIDTH, 128), F32)

    def assemble_wide(phase, source, first, second):
        def body(group):
            for down, across, indices in places(group, -1):
                firsts, seconds = [], []
                for at in indices:
                    one, two = merge(source[at].astype(F32), source[at + COLS].astype(F32))
                    firsts.append(one)
                    seconds.append(two)
                first[down, across] = jnp.concatenate(firsts + [empty], axis=0).astype(BF16)
                second[down, across] = jnp.concatenate(seconds + [empty], axis=0).astype(BF16)

        receive(phase, send_wide, source, body)

    def open_slim(source, at):
        rows = source[at].astype(F32).reshape(TILES, 128)
        return jnp.concatenate([rows, jnp.zeros((4, 128), F32)], axis=0)

    def assemble_slim(phase, source, target):
        def body(group):
            low = lax.broadcasted_iota(jnp.int32, (8, 128), 0) < 4
            for down, across, indices in places(group, -1):
                parts = []
                for at in indices:
                    one, two = merge(open_slim(source, at), open_slim(source, at + COLS))
                    last = jnp.where(low, one[8:16], pltpu.roll(two[8:16], 4, axis=0))
                    parts += [one[0:8], two[0:8], last]
                target[down, across] = jnp.concatenate(parts + [empty], axis=0).astype(BF16)

        receive(phase, send_slim, source, body)

    def split_wide(phase, first, second, target):
        def body(group):
            for down, across, indices in places(group, 1):
                lower, upper = merge(first[down, across], second[down, across])
                for part, at in enumerate(indices):
                    cut = slice(part * WIDTH, (part + 1) * WIDTH)
                    send_wide[at] = lower[cut].astype(BF16)
                    send_wide[at + COLS] = upper[cut].astype(BF16)
            send(phase, send_wide, target, group)

        send_all(body)

    def split_slim(phase, source, target):
        def body(group):
            for down, across, indices in places(group, 1):
                values = source[down, across]
                for part, at in enumerate(indices):
                    cut = values[part * WIDTH : (part + 1) * WIDTH]
                    last = cut[16:24]
                    low_0, low_1 = merge(cut[0:8], cut[8:16])
                    high_0, high_1 = merge(last, pltpu.roll(last, 4, axis=0))
                    for to, lines in ((at, (low_0, high_0)), (at + COLS, (low_1, high_1))):
                        rows = jnp.concatenate([lines[0], lines[1][0:4]], axis=0)
                        send_slim[to] = rows.astype(BF16).reshape(3, 4, 128)
            send(phase, send_slim, target, group)

        send_all(body)

    greet(1, 30)
    loads[0].wait()
    load_block(block, state, lambda tile: greet(30 + tile * 8, 38 + tile * 8))
    greet(126, DEVICES)
    def prepare(u):
        weight_t[u] = iw_ref[u].astype(F32).T.astype(BF16)
        out_weight_t[u] = ow_ref[u].astype(F32).T.astype(BF16)
        for i, ref in ((u, ig_ref), (2 + u, og_ref)):
            spread = jnp.broadcast_to(ref[u : u + 1, :], (CH, CH)).T
            gains[i] = jnp.concatenate([spread, spread], axis=1)

    loads[1].wait()
    loads[2].wait()
    prepare(0)
    steps(lambda s, at: project(0, s, at, state[:, at]))
    pl.semaphore_wait(barrier, DEVICES - 1)
    send_swap(0, send_wide, wide_0, WIDTH)
    prepare(1)
    loads[3].wait()
    load_block(ct_ref, upstream)
    assemble_wide(0, wide_0, left.at[0], right.at[0])
    result[0] = dot(right[0], left[0], 0, 0)
    split_slim(1, result.at[0], slim_0)
    steps(lambda s, at: gates(0, s, at))
    steps(lambda s, at: factors(0, s, at))
    receive_swap(1, send_slim, slim_0, TILES)

    def middle(s, at):
        project(1, s, at, finish(0, s, at)[0])

    steps(middle)
    send_swap(2, send_wide, wide_1, WIDTH)
    steps(lambda s, at: gates(1, s, at))
    steps(early)
    assemble_wide(2, wide_1, left.at[1], right.at[1])
    result[0] = dot(right[1], left[1], 1, 1)
    split_slim(3, result.at[0], slim_1)
    steps(lambda s, at: factors(1, s, at))
    receive_swap(3, send_slim, slim_1, TILES)

    def top(s, at):
        _, normed, inverse, values, gate = finish(1, s, at)
        finish_back(1, s, at, upstream[:, at], normed, inverse, values, gate, early_back[:, at])

    steps(top)
    send_swap(4, send_slim, slim_2, TILES)
    store_block(state, flat)
    block[...] = flat[...].astype(BF16)
    store = pltpu.make_async_copy(block, out_hbm, copy_sem.at[0])
    store.start()
    assemble_slim(4, slim_2, grad)
    result[0] = dot(grad[...], right[1], 0, 0)
    result[1] = dot(grad[...], left[1], 1, 0)
    split_wide(5, result.at[0], result.at[1], wide_2)
    receive_swap(5, send_wide, wide_2, WIDTH)

    def bottom(s, at):
        up = project_back(1, s, at)
        gate = mixed[0, 4 * CH :, at]
        finish_back(
            0,
            s,
            at,
            up,
            norm_out[0, :, at],
            inverse_out[0, :, at],
            projected[0, :, at],
            gate,
        )

    steps(bottom)
    send_swap(6, send_slim, slim_3, TILES)
    assemble_slim(6, slim_3, grad)
    result[0] = dot(right[0], grad[...], 1, 0)
    result[1] = dot(left[0], grad[...], 1, 1)
    split_wide(7, result.at[0], result.at[1], wide_3)
    receive_swap(7, send_wide, wide_3, WIDTH)

    steps(lambda s, at: project_back(0, s, at))
    store_block(upstream, flat)
    final = pltpu.make_async_copy(flat, grad_hbm, copy_sem.at[1])
    final.start()
    store.wait()
    final.wait()


def local(
    pair_input, chain_lengths, input_gain, input_weight, output_gain, output_weight, cotangent
):
    cells = HEIGHT * WIDTH
    vmem = pl.BlockSpec(memory_space=pltpu.VMEM)
    hbm = pl.BlockSpec(memory_space=pltpu.HBM)
    free = pl.BlockSpec(memory_space=pl.ANY)
    smem = pl.BlockSpec(memory_space=pltpu.SMEM)
    wide = pltpu.VMEM((DEVICES, WIDTH, 128), BF16)
    slim = pltpu.VMEM((DEVICES, 3, 4, 128), BF16)
    plane = pltpu.VMEM((CH, LANES), F32)
    planes = pltpu.VMEM((2, CH, LANES), F32)
    line = pltpu.VMEM((2, 1, LANES), F32)
    out, grad = pl.pallas_call(
        kernel,
        out_shape=(
            jax.ShapeDtypeStruct((cells, CH), BF16),
            jax.ShapeDtypeStruct((cells, CH), F32),
        ),
        in_specs=[hbm, smem, vmem, hbm, vmem, hbm, hbm],
        out_specs=(free, free),
        scratch_shapes=[
            pltpu.VMEM((cells, CH), BF16),
            pltpu.VMEM((2, CH, 5 * CH), BF16),
            pltpu.VMEM((2, CH, CH), BF16),
            pltpu.VMEM((cells, CH), BF16),
            pltpu.VMEM((cells, CH), F32),
            plane,
            plane,
            pltpu.VMEM((2, 5 * CH, LANES), F32),
            planes,
            line,
            planes,
            line,
            planes,
            plane,
            pltpu.VMEM((CH * WIDTH, 128), F32),
            pltpu.VMEM((CH * WIDTH, 128), F32),
            pltpu.VMEM((4, CH, STEP), F32),
            pltpu.VMEM((2, 5 * CH, CH), BF16),
            pltpu.VMEM((2, CH, CH), BF16),
            pltpu.VMEM((2, SIDE, SIDE), BF16),
            pltpu.VMEM((2, SIDE, SIDE), BF16),
            pltpu.VMEM((SIDE, SIDE), BF16),
            pltpu.VMEM((2, SIDE, SIDE), F32),
            wide,
            slim,
            wide,
            wide,
            wide,
            wide,
            slim,
            slim,
            slim,
            slim,
            pltpu.SemaphoreType.DMA((8,)),
            pltpu.SemaphoreType.DMA((8, CHAINS)),
            pltpu.SemaphoreType.DMA((4,)),
        ],
        compiler_params=pltpu.CompilerParams(
            collective_id=0, has_side_effects=True, vmem_limit_bytes=52 * 2**20
        ),
    )(
        pair_input.reshape(cells, CH),
        chain_lengths,
        input_gain,
        input_weight,
        output_gain,
        output_weight,
        cotangent.reshape(cells, CH),
    )
    shape = (HEIGHT, WIDTH, CH)
    return out.reshape(shape), grad.reshape(shape)


def solution(mesh):
    placed = (P("row", "col", None), P(), P(), P(), P(), P(), P("row", "col", None))
    return jax.shard_map(
        local,
        mesh=mesh,
        in_specs=placed,
        out_specs=(P("row", "col", None), P("row", "col", None)),
        check_vma=False,
    )
```

```python
import functools

import jax
import jax.numpy as jnp
from jax import lax
from jax.experimental import pallas as pl
from jax.experimental.pallas import tpu as pltpu
from jax.sharding import PartitionSpec as P

MESH = pl.DeviceIdType.MESH
F32 = jnp.float32
BF16 = jnp.bfloat16

CH = 128
N = 384
CHAINS = 8
EPSILON = 1e-05

ROWS, COLS = 8, 16
DEVICES = ROWS * COLS
HEIGHT, WIDTH = N // ROWS, N // COLS
HALF = 64
TILES = WIDTH // 2
LANES = TILES * 128
STEP = 256
STEPS = LANES // STEP
SIDE = CHAINS * HALF


UNITS = (
    (20842, 2390, 4165),
    (64490, 1022, 4164),
    (325, 6122, 17489),
    (1007, 15690, 1105),
)


def column_pair(tile):
    return (tile, tile + 8) if tile < 8 else (tile + 8, tile + 12)


def sigmoid(values):
    return 0.5 * jnp.tanh(0.5 * values) + 0.5


def mean_rows(values):
    return jnp.sum(values, axis=0, keepdims=True) * (1.0 / values.shape[0])


def normalize(values):
    center = values - mean_rows(values)
    inverse = lax.rsqrt(mean_rows(center * center) + EPSILON)
    return center * inverse, inverse


def norm_backward(grad_normed, normed, inverse):
    return inverse * (
        grad_normed - mean_rows(grad_normed) - normed * mean_rows(grad_normed * normed)
    )


def dot(first, second, first_dim=1, second_dim=0):
    return lax.dot_general(
        first, second, (((first_dim,), (second_dim,)), ((), ())), preferred_element_type=F32
    )


def swap_halves(values):
    return pltpu.roll(values, HALF, axis=len(values.shape) - 1)


def lower_lanes(shape):
    return lax.broadcasted_iota(jnp.int32, shape, len(shape) - 1) % 128 < HALF


def half_lane():
    return lax.broadcasted_iota(jnp.int32, (8, 128), 1) % HALF


def upper_rows():
    return lax.broadcasted_iota(jnp.int32, (8, 128), 0) < 4


def fold(values):
    first, second, last = values[0:8], values[8:16], values[16:24]
    spare, low = half_lane() >= HEIGHT, upper_rows()
    turned = pltpu.roll(last, 4, axis=0)
    extra = jnp.where(low, pltpu.roll(turned, 48, axis=1), pltpu.roll(last, 32, axis=1))
    first = jnp.where(spare, extra, first)
    second = jnp.where(spare & low, pltpu.roll(turned, 16, axis=1), second)
    return jnp.concatenate([first, second, last[0:4]], axis=0)


def unfold(values):
    first, second = values[0:8], values[8:16]
    lane, low = half_lane(), upper_rows()
    ends = jnp.where(lane < 16, pltpu.roll(first, 80, axis=1), pltpu.roll(second, 112, axis=1))
    middle = (lane >= 16) & (lane < 32)
    last = jnp.where(middle, pltpu.roll(first, 96, axis=1), pltpu.roll(ends, 4, axis=0))
    kept = lane < HEIGHT
    last = jnp.where(kept, last, 0.0)
    held = jnp.concatenate([values[16:20], jnp.zeros((4, 128), F32)], axis=0)
    return jnp.concatenate(
        [jnp.where(kept, first, 0.0), jnp.where(kept, second, 0.0), jnp.where(low, held, last)],
        axis=0,
    )


def merge(first, second):
    lower = lower_lanes(first.shape)
    return (
        jnp.where(lower, first, swap_halves(second)),
        jnp.where(lower, swap_halves(first), second),
    )


def kernel(
    x_hbm,
    length_ref,
    ig_ref,
    iw_hbm,
    og_ref,
    ow_hbm,
    ct_hbm,
    out_hbm,
    grad_hbm,
    block,
    iw_ref,
    ow_ref,
    ct_ref,
    flat,
    state,
    upstream,
    mixed,
    norm_in,
    inverse_in,
    norm_out,
    inverse_out,
    projected,
    early_back,
    swap,
    inbox,
    gains,
    weight_t,
    out_weight_t,
    left,
    right,
    grad,
    result,
    send_wide,
    send_slim,
    wide_0,
    wide_1,
    wide_2,
    wide_3,
    slim_0,
    slim_1,
    slim_2,
    slim_3,
    send_sem,
    recv_sem,
    copy_sem,
):
    row, col = lax.axis_index("row"), lax.axis_index("col")
    me = row * COLS + col
    my_chain = col // 2
    my_pair = row // 2

    loads = [
        pltpu.make_async_copy(source, target, copy_sem.at[i])
        for i, (source, target) in enumerate(
            ((x_hbm, block), (iw_hbm, iw_ref), (ow_hbm, ow_ref), (ct_hbm, ct_ref))
        )
    ]
    for copy in loads:
        copy.start()

    barrier = pltpu.get_barrier_semaphore()

    def greet(first, last):
        for t in range(first, last):
            peer = (lax.rem(row + t // COLS, ROWS), lax.rem(col + t % COLS, COLS))
            pl.semaphore_signal(barrier, inc=1, device_id=peer, device_id_type=MESH)

    def units_of(group, sign):
        for offsets in UNITS:
            x, z, y = [(bits >> (2 * group)) & 3 for bits in offsets]
            pair = (my_pair + sign * z) & 3
            chain = ((my_chain // 2 + sign * x) & 3) * 2 + (my_chain + y) % 2
            yield pair, chain

    def send(phase, source, target, group):
        for unit, (pair, chain) in enumerate(units_of(group, 1)):
            for low in range(2):
                for part in range(2):
                    peer = (pair * 2 + lax.rem(row + low, 2), chain * 2 + part)
                    at = peer[0] * COLS + peer[1]

                    def start(peer=peer, at=at):
                        pltpu.make_async_remote_copy(
                            source.at[at],
                            target.at[me],
                            send_sem.at[phase],
                            recv_sem.at[phase, group],
                            device_id=peer,
                            device_id_type=MESH,
                        ).start()

                    if unit < 3 or low > 0:
                        start()
                    else:

                        @pl.when(at != me)
                        def _():
                            start()

                        @pl.when(at == me)
                        def _():
                            target[me] = source[me]

    def send_all(body):
        def one(s, carry):
            body(s)
            return carry

        lax.fori_loop(0, CHAINS, one, 0)

    def receive(phase, source, target, body):
        def arrived(count):
            some = pl.ds(0, count)
            return pltpu.make_async_remote_copy(
                source.at[some],
                target.at[some],
                send_sem.at[phase],
                recv_sem.at[phase, 0],
                device_id=(row, col),
                device_id_type=MESH,
            )

        def one(group, carry):
            def wait(count):
                some = pl.ds(0, count)
                pltpu.make_async_remote_copy(
                    source.at[some],
                    target.at[some],
                    send_sem.at[phase],
                    recv_sem.at[phase, group],
                    device_id=(row, col),
                    device_id_type=MESH,
                ).wait_recv()

            @pl.when(group == CHAINS - 1)
            def _():
                wait(2 * ROWS - 1)

            @pl.when(group < CHAINS - 1)
            def _():
                wait(2 * ROWS)

            body(group)
            return carry

        lax.fori_loop(0, CHAINS, one, 0)
        arrived(DEVICES - 1).wait_send()

    def steps(body):
        def one(s, carry):
            body(s, pl.ds(pl.multiple_of(s * STEP, STEP), STEP))
            return carry

        lax.fori_loop(0, STEPS, one, 0, unroll=True)

    def tiles_of(s):
        pairs = []
        for i in range(2):
            tile = s * 2 + i
            late = tile >= 8
            pairs.append((tile + jnp.where(late, 8, 0), tile + jnp.where(late, 12, 8)))
        return pairs

    def valid(s):
        lane = lax.broadcasted_iota(jnp.int32, (1, STEP), 1) + s * STEP
        tile = lane // 128
        token = lane % HALF
        upper = (lane // HALF) % 2
        column = tile + jnp.where(tile < 8, 8 * upper, 8 + 4 * upper) + (col % 2) * WIDTH
        inside = (token < length_ref[row]) & (column < length_ref[my_chain])
        return jnp.where(inside, 1.0, 0.0)

    def load_block(source, target, beside=lambda tile: None):
        flat[...] = source[...].astype(F32)
        empty = jnp.zeros((HALF - HEIGHT, CH), F32)
        for tile in range(TILES):
            parts = []
            for column in column_pair(tile):
                parts += [flat[pl.ds(column, HEIGHT, stride=WIDTH), :], empty]
            target[:, tile * 128 : (tile + 1) * 128] = jnp.concatenate(parts, axis=0).T
            beside(tile)

    def store_block(source, target):
        for tile in range(TILES):
            values = source[:, tile * 128 : (tile + 1) * 128].T
            for half, column in enumerate(column_pair(tile)):
                target[pl.ds(column, HEIGHT, stride=WIDTH), :] = values[
                    half * HALF : half * HALF + HEIGHT
                ]

    def put_wide(s, first, second):
        for i, (one, two) in enumerate(tiles_of(s)):
            at = slice(i * 128, (i + 1) * 128)
            lower, upper = merge(first[:, at], second[:, at])
            swap[pl.ds(one, CH, stride=WIDTH), :] = lower
            swap[pl.ds(two, CH, stride=WIDTH), :] = upper

    def get_wide(s):
        firsts, seconds = [], []
        for one, two in tiles_of(s):
            lower, upper = merge(
                inbox[pl.ds(one, CH, stride=WIDTH), :], inbox[pl.ds(two, CH, stride=WIDTH), :]
            )
            firsts.append(lower)
            seconds.append(upper)
        return jnp.concatenate(firsts, axis=1), jnp.concatenate(seconds, axis=1)

    def put_slim(s, values):
        for i in range(2):
            swap[pl.ds(s * 2 + i, CH, stride=TILES), :] = values[:, i * 128 : (i + 1) * 128]

    def get_slim(s):
        return jnp.concatenate(
            [inbox[pl.ds(s * 2 + i, CH, stride=TILES), :] for i in range(2)], axis=1
        )

    def channels_of(group, sign, rows):
        for pair, chain in units_of(group, sign):
            for low in range(2):
                at = (pair * 2 + low) * COLS + chain * 2
                yield pl.ds(at, 2), pl.ds(pl.multiple_of(at * rows, 2 * rows), 2 * rows)

    def put_folded(target, at, values):
        target[at] = fold(values).astype(BF16).reshape(5, 4, 128)

    def get_folded(source, at):
        return unfold(source[at].astype(F32).reshape(20, 128))

    def send_swap(phase, source, target, rows):
        def body(group):
            for messages, at in channels_of(group, 1, rows):
                if rows == WIDTH:
                    values = swap[at, :]
                    for i in range(2):
                        put_folded(source, messages.start + i, values[i * rows : (i + 1) * rows])
                else:
                    source[messages] = swap[at, :].astype(BF16).reshape((2,) + source.shape[1:])
            send(phase, source, target, group)

        send_all(body)

    def receive_swap(phase, source, target, rows):
        def body(group):
            for messages, at in channels_of(group, -1, rows):
                if rows == WIDTH:
                    parts = [get_folded(target, messages.start + i) for i in range(2)]
                    inbox[at, :] = jnp.concatenate(parts, axis=0)
                else:
                    inbox[at, :] = target[messages].astype(F32).reshape(2 * rows, 128)

        receive(phase, source, target, body)

    def project(u, s, at, values):
        normed, inverse = normalize(values)
        norm_in[u, :, at] = normed
        inverse_in[u, :, at] = inverse
        mix = dot(weight_t[u], (normed * gains[u]).astype(BF16))
        mixed[u, :, at] = mix
        keep = valid(s)
        put_wide(
            s,
            sigmoid(mix[CH : 2 * CH]) * mix[0:CH] * keep,
            sigmoid(mix[3 * CH : 4 * CH]) * mix[2 * CH : 3 * CH] * keep,
        )

    def finish(u, s, at):
        normed, inverse = normalize(get_slim(s))
        norm_out[u, :, at] = normed
        inverse_out[u, :, at] = inverse
        values = dot(out_weight_t[u], (normed * gains[2 + u]).astype(BF16))
        projected[u, :, at] = values
        gate = mixed[u, 4 * CH :, at]
        after = (state[:, at] + gate * values).astype(BF16).astype(F32)
        state[:, at] = after
        return after, normed, inverse, values, gate

    def scaled_back(u, at, grad_projected):
        return dot(ow_ref[u], grad_projected.astype(BF16)) * gains[2 + u]

    def early(s, at):
        early_back[:, at] = scaled_back(1, at, upstream[:, at] * mixed[1, 4 * CH :, at])

    def finish_back(u, s, at, up, normed, inverse, values, gate, grad_scaled=None):
        grad_projected = up * gate
        mixed[u, 4 * CH :, at] = grad_projected * values * (1.0 - gate)
        if grad_scaled is None:
            grad_scaled = scaled_back(u, at, grad_projected)
        put_slim(s, norm_backward(grad_scaled, normed, inverse))

    def gates(u, s, at):
        mixed[u, 4 * CH :, at] = sigmoid(mixed[u, 4 * CH :, at])

    def factors(u, s, at):
        keep = valid(s)
        for base in (0, 2 * CH):
            gate = sigmoid(mixed[u, base + CH : base + 2 * CH, at])
            kept = gate * keep
            mixed[u, base : base + CH, at] = mixed[u, base : base + CH, at] * kept * (1.0 - gate)
            mixed[u, base + CH : base + 2 * CH, at] = kept

    def project_back(u, s, at):
        parts = []
        for values, base in zip(get_wide(s), (0, 2 * CH)):
            parts.append((values * mixed[u, base + CH : base + 2 * CH, at]).astype(BF16))
            parts.append((values * mixed[u, base : base + CH, at]).astype(BF16))
        parts.append(mixed[u, 4 * CH :, at].astype(BF16))
        grad_scaled = dot(iw_ref[u], jnp.concatenate(parts, axis=0))
        after = upstream[:, at] + norm_backward(
            grad_scaled * gains[u], norm_in[u, :, at], inverse_in[u, :, at]
        )
        upstream[:, at] = after
        return after

    def places(group, sign):
        for pair, chain in units_of(group, sign):
            yield (
                pl.ds(pl.multiple_of(chain * HALF, HALF), HALF),
                pl.ds(pl.multiple_of(pair * 128, 128), 128),
                [pair * 2 * COLS + chain * 2 + part for part in range(2)],
            )

    empty = jnp.zeros((HALF - 2 * WIDTH, 128), F32)

    def assemble_wide(phase, source, first, second):
        def body(group):
            for down, across, indices in places(group, -1):
                firsts, seconds = [], []
                for at in indices:
                    one, two = merge(get_folded(source, at), get_folded(source, at + COLS))
                    firsts.append(one)
                    seconds.append(two)
                first[down, across] = jnp.concatenate(firsts + [empty], axis=0).astype(BF16)
                second[down, across] = jnp.concatenate(seconds + [empty], axis=0).astype(BF16)

        receive(phase, send_wide, source, body)

    def open_slim(source, at):
        rows = source[at].astype(F32).reshape(TILES, 128)
        return jnp.concatenate([rows, jnp.zeros((4, 128), F32)], axis=0)

    def assemble_slim(phase, source, target):
        def body(group):
            low = lax.broadcasted_iota(jnp.int32, (8, 128), 0) < 4
            for down, across, indices in places(group, -1):
                parts = []
                for at in indices:
                    one, two = merge(open_slim(source, at), open_slim(source, at + COLS))
                    last = jnp.where(low, one[8:16], pltpu.roll(two[8:16], 4, axis=0))
                    parts += [one[0:8], two[0:8], last]
                target[down, across] = jnp.concatenate(parts + [empty], axis=0).astype(BF16)

        receive(phase, send_slim, source, body)

    def split_wide(phase, first, second, target):
        def body(group):
            for down, across, indices in places(group, 1):
                lower, upper = merge(first[down, across], second[down, across])
                for part, at in enumerate(indices):
                    cut = slice(part * WIDTH, (part + 1) * WIDTH)
                    put_folded(send_wide, at, lower[cut])
                    put_folded(send_wide, at + COLS, upper[cut])
            send(phase, send_wide, target, group)

        send_all(body)

    def split_slim(phase, source, target):
        def body(group):
            for down, across, indices in places(group, 1):
                values = source[down, across]
                for part, at in enumerate(indices):
                    cut = values[part * WIDTH : (part + 1) * WIDTH]
                    last = cut[16:24]
                    low_0, low_1 = merge(cut[0:8], cut[8:16])
                    high_0, high_1 = merge(last, pltpu.roll(last, 4, axis=0))
                    for to, lines in ((at, (low_0, high_0)), (at + COLS, (low_1, high_1))):
                        rows = jnp.concatenate([lines[0], lines[1][0:4]], axis=0)
                        send_slim[to] = rows.astype(BF16).reshape(3, 4, 128)
            send(phase, send_slim, target, group)

        send_all(body)

    greet(1, 30)
    loads[0].wait()
    load_block(block, state, lambda tile: greet(30 + tile * 8, 38 + tile * 8))
    greet(126, DEVICES)
    def prepare(u):
        weight_t[u] = iw_ref[u].astype(F32).T.astype(BF16)
        out_weight_t[u] = ow_ref[u].astype(F32).T.astype(BF16)
        for i, ref in ((u, ig_ref), (2 + u, og_ref)):
            spread = jnp.broadcast_to(ref[u : u + 1, :], (CH, CH)).T
            gains[i] = jnp.concatenate([spread, spread], axis=1)

    loads[1].wait()
    loads[2].wait()
    prepare(0)
    steps(lambda s, at: project(0, s, at, state[:, at]))
    pl.semaphore_wait(barrier, DEVICES - 1)
    send_swap(0, send_wide, wide_0, WIDTH)
    prepare(1)
    loads[3].wait()
    load_block(ct_ref, upstream)
    assemble_wide(0, wide_0, left.at[0], right.at[0])
    result[0] = dot(right[0], left[0], 0, 0)
    split_slim(1, result.at[0], slim_0)
    steps(lambda s, at: gates(0, s, at))
    steps(lambda s, at: factors(0, s, at))
    receive_swap(1, send_slim, slim_0, TILES)

    def middle(s, at):
        project(1, s, at, finish(0, s, at)[0])

    steps(middle)
    send_swap(2, send_wide, wide_1, WIDTH)
    steps(lambda s, at: gates(1, s, at))
    steps(early)
    assemble_wide(2, wide_1, left.at[1], right.at[1])
    result[0] = dot(right[1], left[1], 1, 1)
    split_slim(3, result.at[0], slim_1)
    steps(lambda s, at: factors(1, s, at))
    receive_swap(3, send_slim, slim_1, TILES)

    def top(s, at):
        _, normed, inverse, values, gate = finish(1, s, at)
        finish_back(1, s, at, upstream[:, at], normed, inverse, values, gate, early_back[:, at])

    steps(top)
    send_swap(4, send_slim, slim_2, TILES)
    store_block(state, flat)
    block[...] = flat[...].astype(BF16)
    store = pltpu.make_async_copy(block, out_hbm, copy_sem.at[0])
    store.start()
    assemble_slim(4, slim_2, grad)
    result[0] = dot(grad[...], right[1], 0, 0)
    result[1] = dot(grad[...], left[1], 1, 0)
    split_wide(5, result.at[0], result.at[1], wide_2)
    receive_swap(5, send_wide, wide_2, WIDTH)

    def bottom(s, at):
        up = project_back(1, s, at)
        gate = mixed[0, 4 * CH :, at]
        finish_back(
            0,
            s,
            at,
            up,
            norm_out[0, :, at],
            inverse_out[0, :, at],
            projected[0, :, at],
            gate,
        )

    steps(bottom)
    send_swap(6, send_slim, slim_3, TILES)
    assemble_slim(6, slim_3, grad)
    result[0] = dot(right[0], grad[...], 1, 0)
    result[1] = dot(left[0], grad[...], 1, 1)
    split_wide(7, result.at[0], result.at[1], wide_3)
    receive_swap(7, send_wide, wide_3, WIDTH)

    steps(lambda s, at: project_back(0, s, at))
    store_block(upstream, flat)
    final = pltpu.make_async_copy(flat, grad_hbm, copy_sem.at[1])
    final.start()
    store.wait()
    final.wait()


def local(
    pair_input, chain_lengths, input_gain, input_weight, output_gain, output_weight, cotangent
):
    cells = HEIGHT * WIDTH
    vmem = pl.BlockSpec(memory_space=pltpu.VMEM)
    hbm = pl.BlockSpec(memory_space=pltpu.HBM)
    free = pl.BlockSpec(memory_space=pl.ANY)
    smem = pl.BlockSpec(memory_space=pltpu.SMEM)
    wide = pltpu.VMEM((DEVICES, 5, 4, 128), BF16)
    slim = pltpu.VMEM((DEVICES, 3, 4, 128), BF16)
    plane = pltpu.VMEM((CH, LANES), F32)
    planes = pltpu.VMEM((2, CH, LANES), F32)
    line = pltpu.VMEM((2, 1, LANES), F32)
    out, grad = pl.pallas_call(
        kernel,
        out_shape=(
            jax.ShapeDtypeStruct((cells, CH), BF16),
            jax.ShapeDtypeStruct((cells, CH), F32),
        ),
        in_specs=[hbm, smem, vmem, hbm, vmem, hbm, hbm],
        out_specs=(free, free),
        scratch_shapes=[
            pltpu.VMEM((cells, CH), BF16),
            pltpu.VMEM((2, CH, 5 * CH), BF16),
            pltpu.VMEM((2, CH, CH), BF16),
            pltpu.VMEM((cells, CH), BF16),
            pltpu.VMEM((cells, CH), F32),
            plane,
            plane,
            pltpu.VMEM((2, 5 * CH, LANES), F32),
            planes,
            line,
            planes,
            line,
            planes,
            plane,
            pltpu.VMEM((CH * WIDTH, 128), F32),
            pltpu.VMEM((CH * WIDTH, 128), F32),
            pltpu.VMEM((4, CH, STEP), F32),
            pltpu.VMEM((2, 5 * CH, CH), BF16),
            pltpu.VMEM((2, CH, CH), BF16),
            pltpu.VMEM((2, SIDE, SIDE), BF16),
            pltpu.VMEM((2, SIDE, SIDE), BF16),
            pltpu.VMEM((SIDE, SIDE), BF16),
            pltpu.VMEM((2, SIDE, SIDE), F32),
            wide,
            slim,
            wide,
            wide,
            wide,
            wide,
            slim,
            slim,
            slim,
            slim,
            pltpu.SemaphoreType.DMA((8,)),
            pltpu.SemaphoreType.DMA((8, CHAINS)),
            pltpu.SemaphoreType.DMA((4,)),
        ],
        compiler_params=pltpu.CompilerParams(
            collective_id=0, has_side_effects=True, vmem_limit_bytes=64 * 2**20 - 64 * 2**10
        ),
    )(
        pair_input.reshape(cells, CH),
        chain_lengths,
        input_gain,
        input_weight,
        output_gain,
        output_weight,
        cotangent.reshape(cells, CH),
    )
    shape = (HEIGHT, WIDTH, CH)
    return out.reshape(shape), grad.reshape(shape)


def solution(mesh):
    placed = (P("row", "col", None), P(), P(), P(), P(), P(), P("row", "col", None))
    return jax.shard_map(
        local,
        mesh=mesh,
        in_specs=placed,
        out_specs=(P("row", "col", None), P("row", "col", None)),
        check_vma=False,
    )
```

```python
import functools

import jax
import jax.numpy as jnp
from jax import lax
from jax.experimental import pallas as pl
from jax.experimental.pallas import tpu as pltpu
from jax.sharding import PartitionSpec as P

MESH = pl.DeviceIdType.MESH
F32 = jnp.float32
BF16 = jnp.bfloat16

CH = 128
N = 384
CHAINS = 8
EPSILON = 1e-05

ROWS, COLS = 8, 16
DEVICES = ROWS * COLS
HEIGHT, WIDTH = N // ROWS, N // COLS
HALF = 64
TILES = WIDTH // 2
LANES = TILES * 128
STEP = 256
STEPS = LANES // STEP
SIDE = CHAINS * HALF


UNITS = (
    (20842, 2390, 4165),
    (64490, 1022, 4164),
    (325, 6122, 17489),
    (1007, 15690, 1105),
)


def distance(offset):
    return -min(offset[0], ROWS - offset[0]) / 2 - min(offset[1], COLS - offset[1]) / 4


FAR_FIRST = sorted(((t // COLS, t % COLS) for t in range(DEVICES)), key=distance)


def column_pair(tile):
    return (tile, tile + 8) if tile < 8 else (tile + 8, tile + 12)


def sigmoid(values):
    return 0.5 * jnp.tanh(0.5 * values) + 0.5


def mean_rows(values):
    return jnp.sum(values, axis=0, keepdims=True) * (1.0 / values.shape[0])


def normalize(values):
    center = values - mean_rows(values)
    inverse = lax.rsqrt(mean_rows(center * center) + EPSILON)
    return center * inverse, inverse


def norm_backward(grad_normed, normed, inverse):
    return inverse * (
        grad_normed - mean_rows(grad_normed) - normed * mean_rows(grad_normed * normed)
    )


def dot(first, second, first_dim=1, second_dim=0):
    return lax.dot_general(
        first, second, (((first_dim,), (second_dim,)), ((), ())), preferred_element_type=F32
    )


def swap_halves(values):
    return pltpu.roll(values, HALF, axis=len(values.shape) - 1)


def lower_lanes(shape):
    return lax.broadcasted_iota(jnp.int32, shape, len(shape) - 1) % 128 < HALF


def half_lane():
    return lax.broadcasted_iota(jnp.int32, (8, 128), 1) % HALF


def upper_rows():
    return lax.broadcasted_iota(jnp.int32, (8, 128), 0) < 4


def fold(values):
    first, second, last = values[0:8], values[8:16], values[16:24]
    spare, low = half_lane() >= HEIGHT, upper_rows()
    turned = pltpu.roll(last, 4, axis=0)
    extra = jnp.where(low, pltpu.roll(turned, 48, axis=1), pltpu.roll(last, 32, axis=1))
    first = jnp.where(spare, extra, first)
    second = jnp.where(spare & low, pltpu.roll(turned, 16, axis=1), second)
    return jnp.concatenate([first, second, last[0:4]], axis=0)


def unfold(values):
    first, second = values[0:8], values[8:16]
    lane, low = half_lane(), upper_rows()
    ends = jnp.where(lane < 16, pltpu.roll(first, 80, axis=1), pltpu.roll(second, 112, axis=1))
    middle = (lane >= 16) & (lane < 32)
    last = jnp.where(middle, pltpu.roll(first, 96, axis=1), pltpu.roll(ends, 4, axis=0))
    kept = lane < HEIGHT
    last = jnp.where(kept, last, 0.0)
    held = jnp.concatenate([values[16:20], jnp.zeros((4, 128), F32)], axis=0)
    return jnp.concatenate(
        [jnp.where(kept, first, 0.0), jnp.where(kept, second, 0.0), jnp.where(low, held, last)],
        axis=0,
    )


def merge(first, second):
    lower = lower_lanes(first.shape)
    return (
        jnp.where(lower, first, swap_halves(second)),
        jnp.where(lower, swap_halves(first), second),
    )


def kernel(
    x_hbm,
    length_ref,
    ig_ref,
    iw_hbm,
    og_ref,
    ow_hbm,
    ct_hbm,
    out_hbm,
    grad_hbm,
    block,
    iw_ref,
    ow_ref,
    ct_ref,
    flat,
    state,
    upstream,
    mixed,
    norm_in,
    inverse_in,
    norm_out,
    inverse_out,
    projected,
    early_back,
    swap,
    inbox,
    gains,
    weight_t,
    out_weight_t,
    left,
    right,
    grad,
    result,
    send_wide,
    send_slim,
    wide_0,
    wide_1,
    wide_2,
    wide_3,
    slim_0,
    slim_1,
    slim_2,
    slim_3,
    send_sem,
    recv_sem,
    copy_sem,
):
    row, col = lax.axis_index("row"), lax.axis_index("col")
    me = row * COLS + col
    my_chain = col // 2
    my_pair = row // 2

    loads = [
        pltpu.make_async_copy(source, target, copy_sem.at[i])
        for i, (source, target) in enumerate(
            ((x_hbm, block), (iw_hbm, iw_ref), (ow_hbm, ow_ref), (ct_hbm, ct_ref))
        )
    ]
    for copy in loads:
        copy.start()

    barrier = pltpu.get_barrier_semaphore()

    def greet(first, last):
        for t in range(first, last):
            down, across = FAR_FIRST[t]
            peer = (lax.rem(row + down, ROWS), lax.rem(col + across, COLS))
            pl.semaphore_signal(barrier, inc=1, device_id=peer, device_id_type=MESH)

    def units_of(group, sign):
        for offsets in UNITS:
            x, z, y = [(bits >> (2 * group)) & 3 for bits in offsets]
            pair = (my_pair + sign * z) & 3
            chain = ((my_chain // 2 + sign * x) & 3) * 2 + (my_chain + y) % 2
            yield pair, chain

    def send(phase, source, target, group):
        for unit, (pair, chain) in enumerate(units_of(group, 1)):
            for low in range(2):
                for part in range(2):
                    peer = (pair * 2 + lax.rem(row + low, 2), chain * 2 + part)
                    at = peer[0] * COLS + peer[1]

                    def start(peer=peer, at=at):
                        pltpu.make_async_remote_copy(
                            source.at[at],
                            target.at[me],
                            send_sem.at[phase],
                            recv_sem.at[phase, group],
                            device_id=peer,
                            device_id_type=MESH,
                        ).start()

                    if unit < 3 or low > 0:
                        start()
                    else:

                        @pl.when(at != me)
                        def _():
                            start()

                        @pl.when(at == me)
                        def _():
                            target[me] = source[me]

    def send_all(body):
        def one(s, carry):
            body(s)
            return carry

        lax.fori_loop(0, CHAINS, one, 0)

    def receive(phase, source, target, body):
        def arrived(count):
            some = pl.ds(0, count)
            return pltpu.make_async_remote_copy(
                source.at[some],
                target.at[some],
                send_sem.at[phase],
                recv_sem.at[phase, 0],
                device_id=(row, col),
                device_id_type=MESH,
            )

        def one(group, carry):
            def wait(count):
                some = pl.ds(0, count)
                pltpu.make_async_remote_copy(
                    source.at[some],
                    target.at[some],
                    send_sem.at[phase],
                    recv_sem.at[phase, group],
                    device_id=(row, col),
                    device_id_type=MESH,
                ).wait_recv()

            @pl.when(group == CHAINS - 1)
            def _():
                wait(2 * ROWS - 1)

            @pl.when(group < CHAINS - 1)
            def _():
                wait(2 * ROWS)

            body(group)
            return carry

        lax.fori_loop(0, CHAINS, one, 0)
        arrived(DEVICES - 1).wait_send()

    def steps(body):
        def one(s, carry):
            body(s, pl.ds(pl.multiple_of(s * STEP, STEP), STEP))
            return carry

        lax.fori_loop(0, STEPS, one, 0, unroll=True)

    def tiles_of(s):
        pairs = []
        for i in range(2):
            tile = s * 2 + i
            late = tile >= 8
            pairs.append((tile + jnp.where(late, 8, 0), tile + jnp.where(late, 12, 8)))
        return pairs

    def valid(s):
        lane = lax.broadcasted_iota(jnp.int32, (1, STEP), 1) + s * STEP
        tile = lane // 128
        token = lane % HALF
        upper = (lane // HALF) % 2
        column = tile + jnp.where(tile < 8, 8 * upper, 8 + 4 * upper) + (col % 2) * WIDTH
        inside = (token < length_ref[row]) & (column < length_ref[my_chain])
        return jnp.where(inside, 1.0, 0.0)

    def load_block(source, target, beside=lambda tile: None):
        flat[...] = source[...].astype(F32)
        empty = jnp.zeros((HALF - HEIGHT, CH), F32)
        for tile in range(TILES):
            parts = []
            for column in column_pair(tile):
                parts += [flat[pl.ds(column, HEIGHT, stride=WIDTH), :], empty]
            target[:, tile * 128 : (tile + 1) * 128] = jnp.concatenate(parts, axis=0).T
            beside(tile)

    def store_block(source, target):
        for tile in range(TILES):
            values = source[:, tile * 128 : (tile + 1) * 128].T
            for half, column in enumerate(column_pair(tile)):
                target[pl.ds(column, HEIGHT, stride=WIDTH), :] = values[
                    half * HALF : half * HALF + HEIGHT
                ]

    def put_wide(s, first, second):
        for i, (one, two) in enumerate(tiles_of(s)):
            at = slice(i * 128, (i + 1) * 128)
            lower, upper = merge(first[:, at], second[:, at])
            swap[pl.ds(one, CH, stride=WIDTH), :] = lower
            swap[pl.ds(two, CH, stride=WIDTH), :] = upper

    def get_wide(s):
        firsts, seconds = [], []
        for one, two in tiles_of(s):
            lower, upper = merge(
                inbox[pl.ds(one, CH, stride=WIDTH), :], inbox[pl.ds(two, CH, stride=WIDTH), :]
            )
            firsts.append(lower)
            seconds.append(upper)
        return jnp.concatenate(firsts, axis=1), jnp.concatenate(seconds, axis=1)

    def put_slim(s, values):
        for i in range(2):
            swap[pl.ds(s * 2 + i, CH, stride=TILES), :] = values[:, i * 128 : (i + 1) * 128]

    def get_slim(s):
        return jnp.concatenate(
            [inbox[pl.ds(s * 2 + i, CH, stride=TILES), :] for i in range(2)], axis=1
        )

    def channels_of(group, sign, rows):
        for pair, chain in units_of(group, sign):
            for low in range(2):
                at = (pair * 2 + low) * COLS + chain * 2
                yield pl.ds(at, 2), pl.ds(pl.multiple_of(at * rows, 2 * rows), 2 * rows)

    def put_folded(target, at, values):
        target[at] = fold(values).astype(BF16).reshape(5, 4, 128)

    def get_folded(source, at):
        return unfold(source[at].astype(F32).reshape(20, 128))

    def send_swap(phase, source, target, rows):
        def body(group):
            for messages, at in channels_of(group, 1, rows):
                if rows == WIDTH:
                    values = swap[at, :]
                    for i in range(2):
                        put_folded(source, messages.start + i, values[i * rows : (i + 1) * rows])
                else:
                    source[messages] = swap[at, :].astype(BF16).reshape((2,) + source.shape[1:])
            send(phase, source, target, group)

        send_all(body)

    def receive_swap(phase, source, target, rows):
        def body(group):
            for messages, at in channels_of(group, -1, rows):
                if rows == WIDTH:
                    parts = [get_folded(target, messages.start + i) for i in range(2)]
                    inbox[at, :] = jnp.concatenate(parts, axis=0)
                else:
                    inbox[at, :] = target[messages].astype(F32).reshape(2 * rows, 128)

        receive(phase, source, target, body)

    def project(u, s, at, values):
        normed, inverse = normalize(values)
        norm_in[u, :, at] = normed
        inverse_in[u, :, at] = inverse
        mix = dot(weight_t[u], (normed * gains[u]).astype(BF16))
        mixed[u, :, at] = mix
        keep = valid(s)
        put_wide(
            s,
            sigmoid(mix[CH : 2 * CH]) * mix[0:CH] * keep,
            sigmoid(mix[3 * CH : 4 * CH]) * mix[2 * CH : 3 * CH] * keep,
        )

    def finish(u, s, at):
        normed, inverse = normalize(get_slim(s))
        norm_out[u, :, at] = normed
        inverse_out[u, :, at] = inverse
        values = dot(out_weight_t[u], (normed * gains[2 + u]).astype(BF16))
        projected[u, :, at] = values
        gate = mixed[u, 4 * CH :, at]
        after = (state[:, at] + gate * values).astype(BF16).astype(F32)
        state[:, at] = after
        return after, normed, inverse, values, gate

    def scaled_back(u, at, grad_projected):
        return dot(ow_ref[u], grad_projected.astype(BF16)) * gains[2 + u]

    def early(s, at):
        early_back[:, at] = scaled_back(1, at, upstream[:, at] * mixed[1, 4 * CH :, at])

    def finish_back(u, s, at, up, normed, inverse, values, gate, grad_scaled=None):
        grad_projected = up * gate
        mixed[u, 4 * CH :, at] = grad_projected * values * (1.0 - gate)
        if grad_scaled is None:
            grad_scaled = scaled_back(u, at, grad_projected)
        put_slim(s, norm_backward(grad_scaled, normed, inverse))

    def gates(u, s, at):
        mixed[u, 4 * CH :, at] = sigmoid(mixed[u, 4 * CH :, at])

    def factors(u, s, at):
        keep = valid(s)
        for base in (0, 2 * CH):
            gate = sigmoid(mixed[u, base + CH : base + 2 * CH, at])
            kept = gate * keep
            mixed[u, base : base + CH, at] = mixed[u, base : base + CH, at] * kept * (1.0 - gate)
            mixed[u, base + CH : base + 2 * CH, at] = kept

    def project_back(u, s, at):
        parts = []
        for values, base in zip(get_wide(s), (0, 2 * CH)):
            parts.append((values * mixed[u, base + CH : base + 2 * CH, at]).astype(BF16))
            parts.append((values * mixed[u, base : base + CH, at]).astype(BF16))
        parts.append(mixed[u, 4 * CH :, at].astype(BF16))
        grad_scaled = dot(iw_ref[u], jnp.concatenate(parts, axis=0))
        after = upstream[:, at] + norm_backward(
            grad_scaled * gains[u], norm_in[u, :, at], inverse_in[u, :, at]
        )
        upstream[:, at] = after
        return after

    def places(group, sign):
        for pair, chain in units_of(group, sign):
            yield (
                pl.ds(pl.multiple_of(chain * HALF, HALF), HALF),
                pl.ds(pl.multiple_of(pair * 128, 128), 128),
                [pair * 2 * COLS + chain * 2 + part for part in range(2)],
            )

    empty = jnp.zeros((HALF - 2 * WIDTH, 128), F32)

    def assemble_wide(phase, source, first, second):
        def body(group):
            for down, across, indices in places(group, -1):
                firsts, seconds = [], []
                for at in indices:
                    one, two = merge(get_folded(source, at), get_folded(source, at + COLS))
                    firsts.append(one)
                    seconds.append(two)
                first[down, across] = jnp.concatenate(firsts + [empty], axis=0).astype(BF16)
                second[down, across] = jnp.concatenate(seconds + [empty], axis=0).astype(BF16)

        receive(phase, send_wide, source, body)

    def open_slim(source, at):
        rows = source[at].astype(F32).reshape(TILES, 128)
        return jnp.concatenate([rows, jnp.zeros((4, 128), F32)], axis=0)

    def assemble_slim(phase, source, target):
        def body(group):
            low = lax.broadcasted_iota(jnp.int32, (8, 128), 0) < 4
            for down, across, indices in places(group, -1):
                parts = []
                for at in indices:
                    one, two = merge(open_slim(source, at), open_slim(source, at + COLS))
                    last = jnp.where(low, one[8:16], pltpu.roll(two[8:16], 4, axis=0))
                    parts += [one[0:8], two[0:8], last]
                target[down, across] = jnp.concatenate(parts + [empty], axis=0).astype(BF16)

        receive(phase, send_slim, source, body)

    def split_wide(phase, first, second, target):
        def body(group):
            for down, across, indices in places(group, 1):
                lower, upper = merge(first[down, across], second[down, across])
                for part, at in enumerate(indices):
                    cut = slice(part * WIDTH, (part + 1) * WIDTH)
                    put_folded(send_wide, at, lower[cut])
                    put_folded(send_wide, at + COLS, upper[cut])
            send(phase, send_wide, target, group)

        send_all(body)

    def split_slim(phase, source, target):
        def body(group):
            for down, across, indices in places(group, 1):
                values = source[down, across]
                for part, at in enumerate(indices):
                    cut = values[part * WIDTH : (part + 1) * WIDTH]
                    last = cut[16:24]
                    low_0, low_1 = merge(cut[0:8], cut[8:16])
                    high_0, high_1 = merge(last, pltpu.roll(last, 4, axis=0))
                    for to, lines in ((at, (low_0, high_0)), (at + COLS, (low_1, high_1))):
                        rows = jnp.concatenate([lines[0], lines[1][0:4]], axis=0)
                        send_slim[to] = rows.astype(BF16).reshape(3, 4, 128)
            send(phase, send_slim, target, group)

        send_all(body)

    greet(0, 40)
    def prepare(u):
        weight_t[u] = iw_ref[u].astype(F32).T.astype(BF16)
        out_weight_t[u] = ow_ref[u].astype(F32).T.astype(BF16)
        for i, ref in ((u, ig_ref), (2 + u, og_ref)):
            spread = jnp.broadcast_to(ref[u : u + 1, :], (CH, CH)).T
            gains[i] = jnp.concatenate([spread, spread], axis=1)

    loads[1].wait()
    loads[2].wait()
    prepare(0)
    greet(40, 67)
    loads[0].wait()
    load_block(block, state, lambda tile: greet(67 + tile * 5, 72 + tile * 5))
    steps(lambda s, at: project(0, s, at, state[:, at]))
    pl.semaphore_wait(barrier, DEVICES - 1)
    send_swap(0, send_wide, wide_0, WIDTH)
    prepare(1)
    loads[3].wait()
    load_block(ct_ref, upstream)
    assemble_wide(0, wide_0, left.at[0], right.at[0])
    result[0] = dot(right[0], left[0], 0, 0)
    split_slim(1, result.at[0], slim_0)
    steps(lambda s, at: gates(0, s, at))
    steps(lambda s, at: factors(0, s, at))
    receive_swap(1, send_slim, slim_0, TILES)

    def middle(s, at):
        project(1, s, at, finish(0, s, at)[0])

    steps(middle)
    send_swap(2, send_wide, wide_1, WIDTH)
    steps(lambda s, at: gates(1, s, at))
    steps(early)
    assemble_wide(2, wide_1, left.at[1], right.at[1])
    result[0] = dot(right[1], left[1], 1, 1)
    split_slim(3, result.at[0], slim_1)
    steps(lambda s, at: factors(1, s, at))
    receive_swap(3, send_slim, slim_1, TILES)

    def top(s, at):
        _, normed, inverse, values, gate = finish(1, s, at)
        finish_back(1, s, at, upstream[:, at], normed, inverse, values, gate, early_back[:, at])

    steps(top)
    send_swap(4, send_slim, slim_2, TILES)
    store_block(state, flat)
    store = pltpu.make_async_copy(flat, out_hbm, copy_sem.at[0])
    store.start()
    assemble_slim(4, slim_2, grad)
    result[0] = dot(grad[...], right[1], 0, 0)
    result[1] = dot(grad[...], left[1], 1, 0)
    split_wide(5, result.at[0], result.at[1], wide_2)
    receive_swap(5, send_wide, wide_2, WIDTH)

    def bottom(s, at):
        up = project_back(1, s, at)
        gate = mixed[0, 4 * CH :, at]
        finish_back(
            0,
            s,
            at,
            up,
            norm_out[0, :, at],
            inverse_out[0, :, at],
            projected[0, :, at],
            gate,
        )

    steps(bottom)
    send_swap(6, send_slim, slim_3, TILES)
    assemble_slim(6, slim_3, grad)
    result[0] = dot(right[0], grad[...], 1, 0)
    result[1] = dot(left[0], grad[...], 1, 1)
    split_wide(7, result.at[0], result.at[1], wide_3)
    receive_swap(7, send_wide, wide_3, WIDTH)

    steps(lambda s, at: project_back(0, s, at))
    store.wait()
    store_block(upstream, flat)
    final = pltpu.make_async_copy(flat, grad_hbm, copy_sem.at[1])
    final.start()
    final.wait()


def local(
    pair_input, chain_lengths, input_gain, input_weight, output_gain, output_weight, cotangent
):
    cells = HEIGHT * WIDTH
    vmem = pl.BlockSpec(memory_space=pltpu.VMEM)
    hbm = pl.BlockSpec(memory_space=pltpu.HBM)
    free = pl.BlockSpec(memory_space=pl.ANY)
    smem = pl.BlockSpec(memory_space=pltpu.SMEM)
    wide = pltpu.VMEM((DEVICES, 5, 4, 128), BF16)
    slim = pltpu.VMEM((DEVICES, 3, 4, 128), BF16)
    plane = pltpu.VMEM((CH, LANES), F32)
    planes = pltpu.VMEM((2, CH, LANES), F32)
    line = pltpu.VMEM((2, 1, LANES), F32)
    out, grad = pl.pallas_call(
        kernel,
        out_shape=(
            jax.ShapeDtypeStruct((cells, CH), F32),
            jax.ShapeDtypeStruct((cells, CH), F32),
        ),
        in_specs=[hbm, smem, vmem, hbm, vmem, hbm, hbm],
        out_specs=(free, free),
        scratch_shapes=[
            pltpu.VMEM((cells, CH), BF16),
            pltpu.VMEM((2, CH, 5 * CH), BF16),
            pltpu.VMEM((2, CH, CH), BF16),
            pltpu.VMEM((cells, CH), BF16),
            pltpu.VMEM((cells, CH), F32),
            plane,
            plane,
            pltpu.VMEM((2, 5 * CH, LANES), F32),
            planes,
            line,
            planes,
            line,
            planes,
            plane,
            pltpu.VMEM((CH * WIDTH, 128), F32),
            pltpu.VMEM((CH * WIDTH, 128), F32),
            pltpu.VMEM((4, CH, STEP), F32),
            pltpu.VMEM((2, 5 * CH, CH), BF16),
            pltpu.VMEM((2, CH, CH), BF16),
            pltpu.VMEM((2, SIDE, SIDE), BF16),
            pltpu.VMEM((2, SIDE, SIDE), BF16),
            pltpu.VMEM((SIDE, SIDE), BF16),
            pltpu.VMEM((2, SIDE, SIDE), F32),
            wide,
            slim,
            wide,
            wide,
            wide,
            wide,
            slim,
            slim,
            slim,
            slim,
            pltpu.SemaphoreType.DMA((8,)),
            pltpu.SemaphoreType.DMA((8, CHAINS)),
            pltpu.SemaphoreType.DMA((4,)),
        ],
        compiler_params=pltpu.CompilerParams(
            collective_id=0, has_side_effects=True, vmem_limit_bytes=64 * 2**20 - 64 * 2**10
        ),
    )(
        pair_input.reshape(cells, CH),
        chain_lengths,
        input_gain,
        input_weight,
        output_gain,
        output_weight,
        cotangent.reshape(cells, CH),
    )
    shape = (HEIGHT, WIDTH, CH)
    return out.astype(BF16).reshape(shape), grad.reshape(shape)


def solution(mesh):
    placed = (P("row", "col", None), P(), P(), P(), P(), P(), P("row", "col", None))
    return jax.shard_map(
        local,
        mesh=mesh,
        in_specs=placed,
        out_specs=(P("row", "col", None), P("row", "col", None)),
        check_vma=False,
    )
```

```python
import functools

import jax
import jax.numpy as jnp
from jax import lax
from jax.experimental import pallas as pl
from jax.experimental.pallas import tpu as pltpu
from jax.sharding import PartitionSpec as P

MESH = pl.DeviceIdType.MESH
F32 = jnp.float32
BF16 = jnp.bfloat16

CH = 128
N = 384
CHAINS = 8
EPSILON = 1e-05

ROWS, COLS = 8, 16
DEVICES = ROWS * COLS
HEIGHT, WIDTH = N // ROWS, N // COLS
HALF = 64
TILES = WIDTH // 2
LANES = TILES * 128
STEP = 256
STEPS = LANES // STEP
SIDE = CHAINS * HALF


UNITS = (
    (20842, 2390, 4165),
    (64490, 1022, 4164),
    (325, 6122, 17489),
    (1007, 15690, 1105),
)


def distance(offset):
    return -min(offset[0], ROWS - offset[0]) / 2 - min(offset[1], COLS - offset[1]) / 4


FAR_FIRST = sorted(((t // COLS, t % COLS) for t in range(DEVICES)), key=distance)


def column_pair(tile):
    return (tile, tile + 8) if tile < 8 else (tile + 8, tile + 12)


def sigmoid(values):
    return 0.5 * jnp.tanh(0.5 * values) + 0.5


def mean_rows(values):
    return jnp.sum(values, axis=0, keepdims=True) * (1.0 / values.shape[0])


def normalize(values):
    center = values - mean_rows(values)
    inverse = lax.rsqrt(mean_rows(center * center) + EPSILON)
    return center * inverse, inverse


def norm_backward(grad_normed, normed, inverse):
    return inverse * (
        grad_normed - mean_rows(grad_normed) - normed * mean_rows(grad_normed * normed)
    )


def dot(first, second, first_dim=1, second_dim=0):
    return lax.dot_general(
        first, second, (((first_dim,), (second_dim,)), ((), ())), preferred_element_type=F32
    )


def swap_halves(values):
    return pltpu.roll(values, HALF, axis=len(values.shape) - 1)


def lower_lanes(shape):
    return lax.broadcasted_iota(jnp.int32, shape, len(shape) - 1) % 128 < HALF


def half_lane():
    return lax.broadcasted_iota(jnp.int32, (8, 128), 1) % HALF


def upper_rows():
    return lax.broadcasted_iota(jnp.int32, (8, 128), 0) < 4


def fold(values):
    first, second, last = values[0:8], values[8:16], values[16:24]
    spare, low = half_lane() >= HEIGHT, upper_rows()
    turned = pltpu.roll(last, 4, axis=0)
    extra = jnp.where(low, pltpu.roll(turned, 48, axis=1), pltpu.roll(last, 32, axis=1))
    first = jnp.where(spare, extra, first)
    second = jnp.where(spare & low, pltpu.roll(turned, 16, axis=1), second)
    return jnp.concatenate([first, second, last[0:4]], axis=0)


def unfold(values):
    first, second = values[0:8], values[8:16]
    lane, low = half_lane(), upper_rows()
    ends = jnp.where(lane < 16, pltpu.roll(first, 80, axis=1), pltpu.roll(second, 112, axis=1))
    middle = (lane >= 16) & (lane < 32)
    last = jnp.where(middle, pltpu.roll(first, 96, axis=1), pltpu.roll(ends, 4, axis=0))
    kept = lane < HEIGHT
    last = jnp.where(kept, last, 0.0)
    held = jnp.concatenate([values[16:20], jnp.zeros((4, 128), F32)], axis=0)
    return jnp.concatenate(
        [jnp.where(kept, first, 0.0), jnp.where(kept, second, 0.0), jnp.where(low, held, last)],
        axis=0,
    )


def merge(first, second):
    lower = lower_lanes(first.shape)
    return (
        jnp.where(lower, first, swap_halves(second)),
        jnp.where(lower, swap_halves(first), second),
    )


def kernel(
    x_hbm,
    length_ref,
    ig_ref,
    iw_hbm,
    og_ref,
    ow_hbm,
    ct_hbm,
    out_hbm,
    grad_hbm,
    block,
    iw_ref,
    ow_ref,
    ct_ref,
    flat,
    state,
    upstream,
    mixed,
    norm_in,
    inverse_in,
    norm_out,
    inverse_out,
    projected,
    early_back,
    swap,
    inbox,
    gains,
    weight_t,
    out_weight_t,
    left,
    right,
    grad,
    result,
    send_wide,
    send_slim,
    wide_0,
    wide_1,
    wide_2,
    wide_3,
    slim_0,
    slim_1,
    slim_2,
    slim_3,
    send_sem,
    recv_sem,
    copy_sem,
):
    row, col = lax.axis_index("row"), lax.axis_index("col")
    me = row * COLS + col
    my_chain = col // 2
    my_pair = row // 2

    loads = [
        pltpu.make_async_copy(source, target, copy_sem.at[i])
        for i, (source, target) in enumerate(
            ((x_hbm, block), (iw_hbm, iw_ref), (ow_hbm, ow_ref), (ct_hbm, ct_ref))
        )
    ]
    for copy in loads:
        copy.start()

    barrier = pltpu.get_barrier_semaphore()

    def greet(first, last):
        for t in range(first, last):
            down, across = FAR_FIRST[t]
            peer = (lax.rem(row + down, ROWS), lax.rem(col + across, COLS))
            pl.semaphore_signal(barrier, inc=1, device_id=peer, device_id_type=MESH)

    def units_of(group, sign):
        for offsets in UNITS:
            x, z, y = [(bits >> (2 * group)) & 3 for bits in offsets]
            pair = (my_pair + sign * z) & 3
            chain = ((my_chain // 2 + sign * x) & 3) * 2 + (my_chain + y) % 2
            yield pair, chain

    def send(phase, source, target, group):
        for unit, (pair, chain) in enumerate(units_of(group, 1)):
            for low in range(2):
                for part in range(2):
                    peer = (pair * 2 + lax.rem(row + low, 2), chain * 2 + part)
                    at = peer[0] * COLS + peer[1]

                    def start(peer=peer, at=at):
                        pltpu.make_async_remote_copy(
                            source.at[at],
                            target.at[me],
                            send_sem.at[phase],
                            recv_sem.at[phase, group],
                            device_id=peer,
                            device_id_type=MESH,
                        ).start()

                    if unit < 3 or low > 0:
                        start()
                    else:

                        @pl.when(at != me)
                        def _():
                            start()

                        @pl.when(at == me)
                        def _():
                            target[me] = source[me]

    def send_all(body):
        def one(s, carry):
            body(s)
            return carry

        lax.fori_loop(0, CHAINS, one, 0)

    def receive(phase, source, target, body):
        def arrived(count):
            some = pl.ds(0, count)
            return pltpu.make_async_remote_copy(
                source.at[some],
                target.at[some],
                send_sem.at[phase],
                recv_sem.at[phase, 0],
                device_id=(row, col),
                device_id_type=MESH,
            )

        def one(group, carry):
            def wait(count):
                some = pl.ds(0, count)
                pltpu.make_async_remote_copy(
                    source.at[some],
                    target.at[some],
                    send_sem.at[phase],
                    recv_sem.at[phase, group],
                    device_id=(row, col),
                    device_id_type=MESH,
                ).wait_recv()

            @pl.when(group == CHAINS - 1)
            def _():
                wait(2 * ROWS - 1)

            @pl.when(group < CHAINS - 1)
            def _():
                wait(2 * ROWS)

            body(group)
            return carry

        lax.fori_loop(0, CHAINS, one, 0)
        arrived(DEVICES - 1).wait_send()

    def steps(body):
        def one(s, carry):
            body(s, pl.ds(pl.multiple_of(s * STEP, STEP), STEP))
            return carry

        lax.fori_loop(0, STEPS, one, 0, unroll=True)

    def tiles_of(s):
        pairs = []
        for i in range(2):
            tile = s * 2 + i
            late = tile >= 8
            pairs.append((tile + jnp.where(late, 8, 0), tile + jnp.where(late, 12, 8)))
        return pairs

    def valid(s):
        lane = lax.broadcasted_iota(jnp.int32, (1, STEP), 1) + s * STEP
        tile = lane // 128
        token = lane % HALF
        upper = (lane // HALF) % 2
        column = tile + jnp.where(tile < 8, 8 * upper, 8 + 4 * upper) + (col % 2) * WIDTH
        inside = (token < length_ref[row]) & (column < length_ref[my_chain])
        return jnp.where(inside, 1.0, 0.0)

    def load_block(source, target, beside=lambda tile: None):
        flat[...] = source[...].astype(F32)
        empty = jnp.zeros((HALF - HEIGHT, CH), F32)
        for tile in range(TILES):
            parts = []
            for column in column_pair(tile):
                parts += [flat[pl.ds(column, HEIGHT, stride=WIDTH), :], empty]
            target[:, tile * 128 : (tile + 1) * 128] = jnp.concatenate(parts, axis=0).T
            beside(tile)

    def store_block(source, target):
        for tile in range(TILES):
            values = source[:, tile * 128 : (tile + 1) * 128].T
            for half, column in enumerate(column_pair(tile)):
                target[pl.ds(column, HEIGHT, stride=WIDTH), :] = values[
                    half * HALF : half * HALF + HEIGHT
                ]

    def put_wide(s, first, second):
        for i, (one, two) in enumerate(tiles_of(s)):
            at = slice(i * 128, (i + 1) * 128)
            lower, upper = merge(first[:, at], second[:, at])
            swap[pl.ds(one, CH, stride=WIDTH), :] = lower
            swap[pl.ds(two, CH, stride=WIDTH), :] = upper

    def get_wide(s):
        firsts, seconds = [], []
        for one, two in tiles_of(s):
            lower, upper = merge(
                inbox[pl.ds(one, CH, stride=WIDTH), :], inbox[pl.ds(two, CH, stride=WIDTH), :]
            )
            firsts.append(lower)
            seconds.append(upper)
        return jnp.concatenate(firsts, axis=1), jnp.concatenate(seconds, axis=1)

    def put_slim(s, values):
        for i in range(2):
            swap[pl.ds(s * 2 + i, CH, stride=TILES), :] = values[:, i * 128 : (i + 1) * 128]

    def get_slim(s):
        return jnp.concatenate(
            [inbox[pl.ds(s * 2 + i, CH, stride=TILES), :] for i in range(2)], axis=1
        )

    def channels_of(group, sign, rows):
        for pair, chain in units_of(group, sign):
            for low in range(2):
                at = (pair * 2 + low) * COLS + chain * 2
                yield pl.ds(at, 2), pl.ds(pl.multiple_of(at * rows, 2 * rows), 2 * rows)

    def put_folded(target, at, values):
        target[at] = fold(values).astype(BF16).reshape(5, 4, 128)

    def get_folded(source, at):
        return unfold(source[at].astype(F32).reshape(20, 128))

    def send_swap(phase, source, target, rows):
        def body(group):
            for messages, at in channels_of(group, 1, rows):
                if rows == WIDTH:
                    values = swap[at, :]
                    for i in range(2):
                        put_folded(source, messages.start + i, values[i * rows : (i + 1) * rows])
                else:
                    source[messages] = swap[at, :].astype(BF16).reshape((2,) + source.shape[1:])
            send(phase, source, target, group)

        send_all(body)

    def receive_swap(phase, source, target, rows):
        def body(group):
            for messages, at in channels_of(group, -1, rows):
                if rows == WIDTH:
                    parts = [get_folded(target, messages.start + i) for i in range(2)]
                    inbox[at, :] = jnp.concatenate(parts, axis=0)
                else:
                    inbox[at, :] = target[messages].astype(F32).reshape(2 * rows, 128)

        receive(phase, source, target, body)

    def project(u, s, at, values):
        normed, inverse = normalize(values)
        norm_in[u, :, at] = normed
        inverse_in[u, :, at] = inverse
        mix = dot(weight_t[u], (normed * gains[u]).astype(BF16))
        mixed[u, :, at] = mix
        keep = valid(s)
        put_wide(
            s,
            sigmoid(mix[CH : 2 * CH]) * mix[0:CH] * keep,
            sigmoid(mix[3 * CH : 4 * CH]) * mix[2 * CH : 3 * CH] * keep,
        )

    def finish(u, s, at):
        normed, inverse = normalize(get_slim(s))
        norm_out[u, :, at] = normed
        inverse_out[u, :, at] = inverse
        values = dot(out_weight_t[u], (normed * gains[2 + u]).astype(BF16))
        projected[u, :, at] = values
        gate = mixed[u, 4 * CH :, at]
        after = (state[:, at] + gate * values).astype(BF16).astype(F32)
        state[:, at] = after
        return after, normed, inverse, values, gate

    def scaled_back(u, at, grad_projected):
        return dot(ow_ref[u], grad_projected.astype(BF16)) * gains[2 + u]

    def early(s, at):
        early_back[:, at] = scaled_back(1, at, upstream[:, at] * mixed[1, 4 * CH :, at])

    def finish_back(u, s, at, up, normed, inverse, values, gate, grad_scaled=None):
        grad_projected = up * gate
        mixed[u, 4 * CH :, at] = grad_projected * values * (1.0 - gate)
        if grad_scaled is None:
            grad_scaled = scaled_back(u, at, grad_projected)
        put_slim(s, norm_backward(grad_scaled, normed, inverse))

    def gates(u, s, at):
        mixed[u, 4 * CH :, at] = sigmoid(mixed[u, 4 * CH :, at])

    def factors(u, s, at):
        keep = valid(s)
        for base in (0, 2 * CH):
            gate = sigmoid(mixed[u, base + CH : base + 2 * CH, at])
            kept = gate * keep
            mixed[u, base : base + CH, at] = mixed[u, base : base + CH, at] * kept * (1.0 - gate)
            mixed[u, base + CH : base + 2 * CH, at] = kept

    def project_back(u, s, at):
        parts = []
        for values, base in zip(get_wide(s), (0, 2 * CH)):
            parts.append((values * mixed[u, base + CH : base + 2 * CH, at]).astype(BF16))
            parts.append((values * mixed[u, base : base + CH, at]).astype(BF16))
        parts.append(mixed[u, 4 * CH :, at].astype(BF16))
        grad_scaled = dot(iw_ref[u], jnp.concatenate(parts, axis=0))
        after = upstream[:, at] + norm_backward(
            grad_scaled * gains[u], norm_in[u, :, at], inverse_in[u, :, at]
        )
        upstream[:, at] = after
        return after

    def places(group, sign):
        for pair, chain in units_of(group, sign):
            yield (
                pl.ds(pl.multiple_of(chain * HALF, HALF), HALF),
                pl.ds(pl.multiple_of(pair * 128, 128), 128),
                [pair * 2 * COLS + chain * 2 + part for part in range(2)],
            )

    empty = jnp.zeros((HALF - 2 * WIDTH, 128), F32)

    def assemble_wide(phase, source, first, second):
        def body(group):
            for down, across, indices in places(group, -1):
                firsts, seconds = [], []
                for at in indices:
                    one, two = merge(get_folded(source, at), get_folded(source, at + COLS))
                    firsts.append(one)
                    seconds.append(two)
                first[down, across] = jnp.concatenate(firsts + [empty], axis=0).astype(BF16)
                second[down, across] = jnp.concatenate(seconds + [empty], axis=0).astype(BF16)

        receive(phase, send_wide, source, body)

    def open_slim(source, at):
        rows = source[at].astype(F32).reshape(TILES, 128)
        return jnp.concatenate([rows, jnp.zeros((4, 128), F32)], axis=0)

    def assemble_slim(phase, source, target):
        def body(group):
            low = lax.broadcasted_iota(jnp.int32, (8, 128), 0) < 4
            for down, across, indices in places(group, -1):
                parts = []
                for at in indices:
                    one, two = merge(open_slim(source, at), open_slim(source, at + COLS))
                    last = jnp.where(low, one[8:16], pltpu.roll(two[8:16], 4, axis=0))
                    parts += [one[0:8], two[0:8], last]
                target[down, across] = jnp.concatenate(parts + [empty], axis=0).astype(BF16)

        receive(phase, send_slim, source, body)

    def split_wide(phase, first, second, target):
        def body(group):
            for down, across, indices in places(group, 1):
                lower, upper = merge(first[down, across], second[down, across])
                for part, at in enumerate(indices):
                    cut = slice(part * WIDTH, (part + 1) * WIDTH)
                    put_folded(send_wide, at, lower[cut])
                    put_folded(send_wide, at + COLS, upper[cut])
            send(phase, send_wide, target, group)

        send_all(body)

    def split_slim(phase, source, target):
        def body(group):
            for down, across, indices in places(group, 1):
                values = source[down, across]
                for part, at in enumerate(indices):
                    cut = values[part * WIDTH : (part + 1) * WIDTH]
                    last = cut[16:24]
                    low_0, low_1 = merge(cut[0:8], cut[8:16])
                    high_0, high_1 = merge(last, pltpu.roll(last, 4, axis=0))
                    for to, lines in ((at, (low_0, high_0)), (at + COLS, (low_1, high_1))):
                        rows = jnp.concatenate([lines[0], lines[1][0:4]], axis=0)
                        send_slim[to] = rows.astype(BF16).reshape(3, 4, 128)
            send(phase, send_slim, target, group)

        send_all(body)

    greet(0, 40)
    def prepare(u):
        weight_t[u] = iw_ref[u].astype(F32).T.astype(BF16)
        out_weight_t[u] = ow_ref[u].astype(F32).T.astype(BF16)
        for i, ref in ((u, ig_ref), (2 + u, og_ref)):
            spread = jnp.broadcast_to(ref[u : u + 1, :], (CH, CH)).T
            gains[i] = jnp.concatenate([spread, spread], axis=1)

    loads[1].wait()
    loads[2].wait()
    prepare(0)
    greet(40, 67)
    loads[0].wait()
    load_block(block, state, lambda tile: greet(67 + tile * 5, 72 + tile * 5))
    steps(lambda s, at: project(0, s, at, state[:, at]))
    pl.semaphore_wait(barrier, DEVICES - 1)
    send_swap(0, send_wide, wide_0, WIDTH)
    prepare(1)
    loads[3].wait()
    load_block(ct_ref, upstream)
    assemble_wide(0, wide_0, left.at[0], right.at[0])
    result[0] = dot(right[0], left[0], 0, 0)
    split_slim(1, result.at[0], slim_0)
    steps(lambda s, at: gates(0, s, at))
    steps(lambda s, at: factors(0, s, at))
    receive_swap(1, send_slim, slim_0, TILES)

    def middle(s, at):
        project(1, s, at, finish(0, s, at)[0])

    steps(middle)
    send_swap(2, send_wide, wide_1, WIDTH)
    steps(lambda s, at: gates(1, s, at))
    steps(early)
    assemble_wide(2, wide_1, left.at[1], right.at[1])
    result[0] = dot(right[1], left[1], 1, 1)
    split_slim(3, result.at[0], slim_1)
    steps(lambda s, at: factors(1, s, at))
    receive_swap(3, send_slim, slim_1, TILES)

    def top(s, at):
        _, normed, inverse, values, gate = finish(1, s, at)
        finish_back(1, s, at, upstream[:, at], normed, inverse, values, gate, early_back[:, at])

    steps(top)
    send_swap(4, send_slim, slim_2, TILES)
    store_block(state, flat)
    store = pltpu.make_async_copy(flat, out_hbm, copy_sem.at[0])
    store.start()
    assemble_slim(4, slim_2, grad)
    result[0] = dot(grad[...], right[1], 0, 0)
    result[1] = dot(grad[...], left[1], 1, 0)
    split_wide(5, result.at[0], result.at[1], wide_2)
    receive_swap(5, send_wide, wide_2, WIDTH)

    def bottom(s, at):
        up = project_back(1, s, at)
        gate = mixed[0, 4 * CH :, at]
        finish_back(
            0,
            s,
            at,
            up,
            norm_out[0, :, at],
            inverse_out[0, :, at],
            projected[0, :, at],
            gate,
        )

    steps(bottom)
    send_swap(6, send_slim, slim_3, TILES)
    assemble_slim(6, slim_3, grad)
    result[0] = dot(right[0], grad[...], 1, 0)
    result[1] = dot(left[0], grad[...], 1, 1)
    split_wide(7, result.at[0], result.at[1], wide_3)
    receive_swap(7, send_wide, wide_3, WIDTH)

    steps(lambda s, at: project_back(0, s, at))
    store.wait()
    store_block(upstream, flat)
    final = pltpu.make_async_copy(flat, grad_hbm, copy_sem.at[1])
    final.start()
    final.wait()


def local(
    pair_input, chain_lengths, input_gain, input_weight, output_gain, output_weight, cotangent
):
    cells = HEIGHT * WIDTH
    vmem = pl.BlockSpec(memory_space=pltpu.VMEM)
    hbm = pl.BlockSpec(memory_space=pltpu.HBM)
    free = pl.BlockSpec(memory_space=pl.ANY)
    smem = pl.BlockSpec(memory_space=pltpu.SMEM)
    wide = pltpu.VMEM((DEVICES + 2, 5, 4, 128), BF16)
    slim = pltpu.VMEM((DEVICES + 2, 3, 4, 128), BF16)
    plane = pltpu.VMEM((CH, LANES), F32)
    planes = pltpu.VMEM((2, CH, LANES), F32)
    line = pltpu.VMEM((2, 1, LANES), F32)
    out, grad = pl.pallas_call(
        kernel,
        out_shape=(
            jax.ShapeDtypeStruct((cells, CH), F32),
            jax.ShapeDtypeStruct((cells, CH), F32),
        ),
        in_specs=[hbm, smem, vmem, hbm, vmem, hbm, hbm],
        out_specs=(free, free),
        scratch_shapes=[
            pltpu.VMEM((cells, CH), BF16),
            pltpu.VMEM((2, CH, 5 * CH), BF16),
            pltpu.VMEM((2, CH, CH), BF16),
            pltpu.VMEM((cells, CH), BF16),
            pltpu.VMEM((cells, CH), F32),
            plane,
            plane,
            pltpu.VMEM((2, 5 * CH, LANES), F32),
            planes,
            line,
            planes,
            line,
            planes,
            plane,
            pltpu.VMEM((CH * WIDTH, 128), F32),
            pltpu.VMEM((CH * WIDTH, 128), F32),
            pltpu.VMEM((4, CH, STEP), F32),
            pltpu.VMEM((2, 5 * CH, CH), BF16),
            pltpu.VMEM((2, CH, CH), BF16),
            pltpu.VMEM((2, SIDE, SIDE), BF16),
            pltpu.VMEM((2, SIDE, SIDE), BF16),
            pltpu.VMEM((SIDE, SIDE), BF16),
            pltpu.VMEM((2, SIDE, SIDE), F32),
            wide,
            slim,
            wide,
            wide,
            wide,
            wide,
            slim,
            slim,
            slim,
            slim,
            pltpu.SemaphoreType.DMA((8,)),
            pltpu.SemaphoreType.DMA((8, CHAINS)),
            pltpu.SemaphoreType.DMA((4,)),
        ],
        compiler_params=pltpu.CompilerParams(
            collective_id=0, has_side_effects=True, vmem_limit_bytes=64 * 2**20 - 64 * 2**10
        ),
    )(
        pair_input.reshape(cells, CH),
        chain_lengths,
        input_gain,
        input_weight,
        output_gain,
        output_weight,
        cotangent.reshape(cells, CH),
    )
    shape = (HEIGHT, WIDTH, CH)
    return out.astype(BF16).reshape(shape), grad.reshape(shape)


def solution(mesh):
    placed = (P("row", "col", None), P(), P(), P(), P(), P(), P("row", "col", None))
    return jax.shard_map(
        local,
        mesh=mesh,
        in_specs=placed,
        out_specs=(P("row", "col", None), P("row", "col", None)),
        check_vma=False,
    )
```
